128 devices in a mesh: tm: 8 (over x_hi, y), chan: 16 (over z, x_lo, core).
Axes of the slice: x: 4 (x_hi: 2, x_lo: 2; x = x_hi * 2 + x_lo), y: 4, z: 4, core: 2. Of those that a mesh axis runs over, the one named last changes fastest.
Arguments:
- voltages: bfloat16 [2048, 131072], P('chan', 'tm'), may hold values from -6 to 6
- filter_taps: float32 [4, 16384], replicated, may hold values from -2 to 2
- delays: int32 [2048], P('chan'), may hold values from 0 to 4095
- dead_inputs: int32 [2048], P('chan'), may hold values 0 or 1
Outputs:
- visibilities: bfloat16 [128, 2048, 2048], P(('tm', 'chan'))
The draws below stay inside these ranges and needn't reach their ends.
All inputs are finite; a program needn't handle non-finite values. No bound on the sum of `dead_inputs` on one device may be relied on, other than what follows from the above.
Results may differ from the reference program's by a relative error of at most 0.0056.
Values may be sent and summed in bfloat16 or wider, within the bound.
A program may use at most 128 MiB of HBM per device.

```python
import jax
import jax.numpy as jnp
from jax import lax

R = 128
NFFT = 16384
TAPS = 4
SIGNALS = 2048
SPECTRA = 8
SAMPLES = 131072
GROUPS = 128
FINE = 64
N_CHAN = 16


def draw_voltages(key, part):
    key_common, key_gain, key_noise = jax.random.split(key, 3)
    common = jax.random.normal(key_common, (1, SAMPLES), jnp.float32)
    gains = jax.random.uniform(key_gain, (SIGNALS, 1), jnp.float32, 0.3, 1.0)
    noise = jax.random.normal(key_noise, (SIGNALS, SAMPLES), jnp.float32)
    values = gains * common + 0.8 * noise
    return jnp.clip(values, -6.0, 6.0).astype(jnp.bfloat16)


def place_ends(array, key, low, high):
    longest = array.shape.index(max(array.shape))
    spots = []
    for shift in (0, 1):
        where = [jax.random.randint(jax.random.fold_in(key, axis), (), 0, length) for axis, length in enumerate(array.shape)]
        where[longest] = (where[longest] + shift) % array.shape[longest]
        spots.append(tuple(where))
    return array.at[spots[0]].set(low).at[spots[1]].set(high)


def centred(key, shape, width, most, kind=jnp.bfloat16):
    entries = width * jax.random.normal(key, shape, jnp.float32)
    return jnp.clip(entries, min=-most, max=most).astype(kind)


def setup_inputs(seed: int = 0) -> dict:
    key_list = jax.random.split(jax.random.key(seed), 5)
    return {
        "voltages": draw_voltages(jax.random.fold_in(key_list[4], 71), 0),
        "filter_taps": centred(key_list[1], (TAPS, NFFT), 0.5, 2.0, jnp.float32),
        "delays": place_ends(jax.random.randint(key_list[2], (SIGNALS,), 0, 4096), jax.random.fold_in(key_list[2], 1), 0, 4095).astype(jnp.int32),
        "dead_inputs": place_ends((jax.random.randint(key_list[3], (SIGNALS,), 0, 8) < 1).astype(jnp.int32), jax.random.fold_in(key_list[3], 1), 0, 1),
    }


two_pi = 6.283185307179586


def dft_tables(radix):
    length = radix * radix
    indices = jnp.arange(radix, dtype=jnp.int32)
    outer = indices[:, None] * indices[None, :]
    angles = (two_pi / radix) * (outer % radix).astype(jnp.float32)
    first_section = jnp.stack([jnp.cos(angles), -jnp.sin(angles)], axis=2).astype(jnp.bfloat16)
    twist = (two_pi / length) * outer.astype(jnp.float32)
    half_cos = jnp.cos(angles[:, : radix // 2])
    half_sin = jnp.sin(angles[:, : radix // 2])
    second_section = jnp.stack([jnp.stack([half_cos, -half_sin], axis=1), jnp.stack([half_sin, half_cos], axis=1)], axis=0).astype(jnp.bfloat16)
    return first_section, jnp.cos(twist), jnp.sin(twist), second_section


def channelise(filtered, delays, dead_inputs, radix):
    signals_here, spectra_here, length = filtered.shape
    first_section, twist_cos, twist_sin, second_section = dft_tables(radix)
    blocks = filtered.reshape(signals_here, spectra_here, radix, radix).astype(jnp.float32)
    partial_sums = jnp.einsum("gtab,akp->gtkpb", blocks, first_section.astype(jnp.float32), precision=lax.Precision.HIGHEST)
    real_part = partial_sums[:, :, :, 0, :]
    imag_part = partial_sums[:, :, :, 1, :]
    turned = jnp.stack([real_part * twist_cos + imag_part * twist_sin, imag_part * twist_cos - real_part * twist_sin], axis=3).astype(jnp.bfloat16)
    spectra = jnp.einsum("gtkpb,pbsm->stmkg", turned.astype(jnp.float32), second_section.astype(jnp.float32), precision=lax.Precision.HIGHEST)
    spectra = spectra.reshape(2, spectra_here, length // 2, signals_here)
    channels = jnp.arange(length // 2, dtype=jnp.int32)
    phases = (two_pi / length) * ((channels[:, None] * delays[None, :]) % length).astype(jnp.float32)
    weight = (1 - dead_inputs).astype(jnp.float32) / radix
    rot_cos = jnp.cos(phases) * weight
    rot_sin = jnp.sin(phases) * weight
    return jnp.stack([spectra[0] * rot_cos - spectra[1] * rot_sin, spectra[0] * rot_sin + spectra[1] * rot_cos], axis=0).astype(jnp.bfloat16)


def fengine(item, filter_taps):
    volt_rows, delays, dead_inputs = item
    signals_here = volt_rows.shape[0]
    own_blocks = volt_rows.reshape(signals_here, SPECTRA, NFFT)
    reach_back = TAPS - 1
    extended = jnp.concatenate([jnp.zeros((signals_here, reach_back, NFFT), jnp.bfloat16), own_blocks], axis=1)
    filtered = filter_taps[0][None, None, :] * extended[:, reach_back:reach_back + SPECTRA].astype(jnp.float32)
    for tap_index in range(1, TAPS):
        filtered = filtered + filter_taps[tap_index][None, None, :] * extended[:, reach_back - tap_index:reach_back - tap_index + SPECTRA].astype(jnp.float32)
    return channelise(filtered.astype(jnp.bfloat16), delays, dead_inputs, R)


def partial_engine(filter_taps):
    def runner(item):
        return fengine(item, filter_taps)
    return runner


def reference(voltages, filter_taps, delays, dead_inputs):
    per_span = SIGNALS // N_CHAN
    spans = (voltages.reshape(N_CHAN, per_span, SAMPLES), delays.reshape(N_CHAN, per_span), dead_inputs.reshape(N_CHAN, per_span))
    spectra = lax.map(partial_engine(filter_taps), spans)

    def correlate(group):
        start = (group * FINE).astype(jnp.int32)
        window = lax.dynamic_slice_in_dim(spectra, start, FINE, axis=3)
        matrix = jnp.transpose(window, (1, 2, 3, 0, 4)).reshape(2 * SPECTRA * FINE, SIGNALS)
        power = jnp.dot(matrix.T, matrix, preferred_element_type=jnp.float32)
        half_rows = SPECTRA * FINE
        cross = jnp.dot(matrix[:half_rows].T, matrix[half_rows:], preferred_element_type=jnp.float32)
        packed = jnp.tril(power) + jnp.triu(cross.T - cross, 1)
        return (packed * (1.0 / (FINE * SPECTRA))).astype(jnp.bfloat16)

    return lax.map(correlate, jnp.arange(GROUPS, dtype=jnp.int32))
```

```python
import functools

import jax
import jax.numpy as jnp
import numpy as np
from jax import lax
from jax.experimental import pallas as pl
from jax.experimental.pallas import tpu as pltpu
from jax.sharding import PartitionSpec as P

R = 128
HALF = R // 2
N_TIME = 8
N_CHAN = 16
MESH = pl.DeviceIdType.MESH
two_pi = 2.0 * np.pi


def dft_tables():
    indices = np.arange(R)
    outer = indices[:, None] * indices[None, :]
    angles = two_pi / R * (outer % R)
    cos, sin = np.cos(angles), np.sin(angles)
    first = np.concatenate([cos, -sin], axis=0)
    twist = two_pi / (R * R) * outer
    cos_m, sin_m = cos[:HALF], sin[:HALF]
    second = np.concatenate(
        [np.concatenate([cos_m, sin_m], axis=1), np.concatenate([-sin_m, cos_m], axis=1)], axis=0
    )
    return (
        jnp.asarray(first, jnp.bfloat16),
        jnp.asarray(np.cos(twist), jnp.float32),
        jnp.asarray(np.sin(twist), jnp.float32),
        jnp.asarray(second, jnp.bfloat16),
    )


def gather_times_kernel(volts, out, send_sem, recv_sem):
    share = out.shape[1]
    tm = lax.axis_index("tm")

    def source(owner):
        return volts.at[pl.ds(owner * share, share)]

    mine = pltpu.make_async_copy(source(tm), out.at[tm], recv_sem)
    mine.start()

    def send(step, carry):
        owner = lax.rem(tm + step, N_TIME)
        pltpu.make_async_remote_copy(
            src_ref=source(owner),
            dst_ref=out.at[tm],
            send_sem=send_sem,
            recv_sem=recv_sem,
            device_id={"tm": owner},
            device_id_type=MESH,
        ).start()
        return carry

    lax.fori_loop(1, N_TIME, send, 0)
    pltpu.make_async_copy(out, out, recv_sem).wait()
    most = out.at[pl.ds(0, N_TIME - 1)]
    pltpu.make_async_copy(most, most, send_sem).wait()


def channelise_kernel(volts, taps, first, twist_cos, twist_sin, second, rot, out, turned_rows):
    share = volts.shape[1]
    n_taps = taps.shape[0]
    low = lax.broadcasted_iota(jnp.int32, (HALF, R), 1) < HALF

    def one_signal(s, carry):
        spectra = []
        for t in range(N_TIME):
            filtered = taps[0] * volts[t, s].astype(jnp.float32)
            for j in range(1, min(n_taps, t + 1)):
                filtered = filtered + taps[j] * volts[t - j, s].astype(jnp.float32)
            sums = jnp.dot(
                first[...], filtered.astype(jnp.bfloat16), preferred_element_type=jnp.float32
            )
            real, imag = sums[:R], sums[R:]
            turned = jnp.concatenate(
                [
                    (real * twist_cos[...] + imag * twist_sin[...]).astype(jnp.bfloat16),
                    (imag * twist_cos[...] - real * twist_sin[...]).astype(jnp.bfloat16),
                ],
                axis=1,
            )
            raw = lax.dot_general(
                second[...],
                turned,
                (((1,), (1,)), ((), ())),
                preferred_element_type=jnp.float32,
            )
            rot_cos, rot_sin = rot[0, s], rot[1, s]
            spectra.append(
                (
                    raw[:HALF] * rot_cos - raw[HALF:] * rot_sin,
                    raw[:HALF] * rot_sin + raw[HALF:] * rot_cos,
                )
            )
            if t % 2 == 1:
                for part in range(2):
                    even, odd = spectra[t - 1][part], spectra[t][part]
                    lower = jnp.where(low, even, pltpu.roll(odd, HALF, 1))
                    upper = jnp.where(low, pltpu.roll(even, HALF, 1), odd)
                    tile = (t // 2) * 2 + part
                    for half, value in enumerate((lower, upper)):
                        row = ((tile * 2 + half) * share + s) * HALF
                        turned_rows[pl.ds(pl.multiple_of(row, HALF), HALF), :] = value
        return carry

    lax.fori_loop(0, share, one_signal, 0)

    def one_channel(m, carry):
        for half in range(2):
            for tile in range(N_TIME):
                base = (tile * 2 + half) * share * HALF
                rows = turned_rows[pl.ds(base + m, share, stride=HALF), :]
                out[2 * m + half, :, tile * R : (tile + 1) * R] = rows.astype(jnp.bfloat16)
        return carry

    lax.fori_loop(0, HALF, one_channel, 0)


def exchange_kernel(spectra, out, send_sem, recv_sem):
    groups, share, _ = spectra.shape
    tm, chan = lax.axis_index("tm"), lax.axis_index("chan")
    me = tm * N_CHAN + chan
    rows = pl.ds(pl.multiple_of((chan * N_TIME + tm) * share, share), share)
    pltpu.make_async_copy(spectra.at[me], out.at[rows], recv_sem).start()

    def send(step, carry):
        group = lax.rem(me + step, groups)
        pltpu.make_async_remote_copy(
            src_ref=spectra.at[group],
            dst_ref=out.at[rows],
            send_sem=send_sem,
            recv_sem=recv_sem,
            device_id={"tm": group // N_CHAN, "chan": lax.rem(group, N_CHAN)},
            device_id_type=MESH,
        ).start()
        return carry

    lax.fori_loop(1, groups, send, 0)
    pltpu.make_async_copy(out, out, recv_sem).wait()
    most = spectra.at[pl.ds(0, groups - 1)]
    pltpu.make_async_copy(most, most, send_sem).wait()


def correlate_kernel(scale, spectra, out, left):
    block = out.shape[0]
    depth = spectra.shape[1]
    i = pl.program_id(0)
    own = spectra[pl.ds(pl.multiple_of(i * block, block), block), :]
    left[0] = own
    for pair in range(depth // (2 * R)):
        real = slice(2 * pair * R, (2 * pair + 1) * R)
        imag = slice((2 * pair + 1) * R, (2 * pair + 2) * R)
        left[1, :, real] = own[:, imag]
        left[1, :, imag] = -own[:, real]

    def product(which, j):
        other = spectra[pl.ds(pl.multiple_of(j * block, block), block), :]
        return lax.dot_general(
            left[which], other, (((1,), (1,)), ((), ())), preferred_element_type=jnp.float32
        )

    def column(j, carry):
        which = (j > i).astype(jnp.int32)
        columns = pl.ds(pl.multiple_of(j * block, block), block)
        out[:, columns] = (product(which, j) * scale).astype(out.dtype)
        return carry

    lax.fori_loop(0, out.shape[1] // block, column, 0)
    shape = (block, block)
    lower = lax.broadcasted_iota(jnp.int32, shape, 0) >= lax.broadcasted_iota(jnp.int32, shape, 1)
    diagonal = pl.ds(pl.multiple_of(i * block, block), block)
    phase = (product(1, i) * scale).astype(out.dtype)
    out[:, diagonal] = jnp.where(lower, out[:, diagonal], phase)


def rotations(delays, dead_inputs):
    fine = two_pi / (R * R) * (delays[:, None] * jnp.arange(R, dtype=jnp.int32) % (R * R)).astype(jnp.float32)
    coarse = two_pi / R * (delays[:, None] * jnp.arange(HALF, dtype=jnp.int32) % R).astype(jnp.float32)
    weight = (1 - dead_inputs).astype(jnp.float32)[:, None] / R
    fine_cos, fine_sin = (jnp.cos(fine) * weight)[:, None, :], (jnp.sin(fine) * weight)[:, None, :]
    coarse_cos, coarse_sin = jnp.cos(coarse)[:, :, None], jnp.sin(coarse)[:, :, None]
    return jnp.stack(
        [coarse_cos * fine_cos - coarse_sin * fine_sin, coarse_sin * fine_cos + coarse_cos * fine_sin],
        axis=0,
    )


def shards(voltages, filter_taps, delays, dead_inputs):
    signals_here = voltages.shape[0]
    share = signals_here // N_TIME
    signals = signals_here * N_CHAN
    groups = N_TIME * N_CHAN
    depth = N_TIME * R
    anywhere = pl.BlockSpec(memory_space=pl.ANY)
    in_vmem = pl.BlockSpec(memory_space=pltpu.VMEM)
    sems = [pltpu.SemaphoreType.DMA, pltpu.SemaphoreType.DMA]

    gathered = pl.pallas_call(
        gather_times_kernel,
        out_shape=jax.ShapeDtypeStruct((N_TIME, share, R, R), jnp.bfloat16),
        in_specs=[anywhere],
        out_specs=anywhere,
        scratch_shapes=sems,
        compiler_params=pltpu.CompilerParams(has_side_effects=True),
        name="gather_times",
    )(voltages.reshape(signals_here, R, R))

    first = lax.axis_index("tm") * share
    rot = rotations(
        lax.dynamic_slice_in_dim(delays, first, share), lax.dynamic_slice_in_dim(dead_inputs, first, share)
    )
    spectra = pl.pallas_call(
        channelise_kernel,
        out_shape=jax.ShapeDtypeStruct((groups, share, depth), jnp.bfloat16),
        in_specs=[in_vmem] * 7,
        out_specs=in_vmem,
        scratch_shapes=[pltpu.VMEM((N_TIME * 2 * share * HALF, R), jnp.float32)],
        compiler_params=pltpu.CompilerParams(vmem_limit_bytes=40 * 2**20),
        name="channelise",
    )(gathered, filter_taps.reshape(-1, R, R), *dft_tables(), rot)

    everyone = pl.pallas_call(
        exchange_kernel,
        out_shape=jax.ShapeDtypeStruct((signals, depth), jnp.bfloat16),
        in_specs=[anywhere],
        out_specs=anywhere,
        scratch_shapes=sems,
        compiler_params=pltpu.CompilerParams(has_side_effects=True),
        name="exchange",
    )(spectra)

    block = 256
    scale = 1.0 / (HALF * N_TIME)
    return pl.pallas_call(
        functools.partial(correlate_kernel, scale),
        grid=(signals // block,),
        out_shape=jax.ShapeDtypeStruct((1, signals, signals), jnp.bfloat16),
        in_specs=[pl.BlockSpec((signals, depth), lambda i: (0, 0), pipeline_mode=pl.Buffered(1))],
        out_specs=pl.BlockSpec((None, block, signals), lambda i: (0, i, 0)),
        scratch_shapes=[pltpu.VMEM((2, block, depth), jnp.bfloat16)],
        compiler_params=pltpu.CompilerParams(vmem_limit_bytes=40 * 2**20),
        name="correlate",
    )(everyone)


def solution(mesh):
    in_specs = (P("chan", "tm"), P(), P("chan"), P("chan"))
    out_specs = P(("tm", "chan"), None, None)
    return jax.shard_map(shards, mesh=mesh, in_specs=in_specs, out_specs=out_specs, check_vma=False)
```

```python
import functools

import jax
import jax.numpy as jnp
import numpy as np
from jax import lax
from jax.experimental import pallas as pl
from jax.experimental.pallas import tpu as pltpu
from jax.sharding import PartitionSpec as P

R = 128
HALF = R // 2
N_TIME = 8
N_CHAN = 16
MESH = pl.DeviceIdType.MESH
two_pi = 2.0 * np.pi


def dft_tables():
    indices = np.arange(R)
    outer = indices[:, None] * indices[None, :]
    angles = two_pi / R * (outer % R)
    cos, sin = np.cos(angles), np.sin(angles)
    first = np.concatenate([cos, -sin], axis=0)
    twist = two_pi / (R * R) * outer
    cos_m, sin_m = cos[:HALF], sin[:HALF]
    second = np.concatenate(
        [np.concatenate([cos_m, sin_m], axis=1), np.concatenate([-sin_m, cos_m], axis=1)], axis=0
    )
    return (
        jnp.asarray(first, jnp.bfloat16),
        jnp.asarray(np.stack([np.cos(twist), np.sin(twist)]), jnp.float32),
        jnp.asarray(second, jnp.bfloat16),
    )


def place():
    tm, chan = lax.axis_index("tm"), lax.axis_index("chan")
    return 2 * (tm // 4) + chan // 2 % 2, tm % 4, chan // 4, chan % 2


def channel_kernel(
    volts, delays_in, dead_in, taps_in, first_in, twist_in, second_in,
    out,
    delays, dead_inputs, raw_taps, first, twist, second,
    own, wide, blocks, times, taps, rot, turned_rows, spectra,
    table_sem, load_sem, send_times, recv_times, send_spectra, recv_spectra,
):
    share = times.shape[1]
    n_taps = raw_taps.shape[0]
    pieces = recv_times.shape[0]
    per = share // pieces
    groups = spectra.shape[0]
    tm, chan = lax.axis_index("tm"), lax.axis_index("chan")

    def partner(step):
        along_y = (3 * step) % 4
        across = step % 2 * (1 - step // 4) + (1 - step % 2) * (step // 4)
        return (tm // 4 + across) % 2 * 4 + (tm + along_y) % 4

    def rows_of(owner):
        return pl.ds(pl.multiple_of(owner * share, share), share)

    def load(step):
        rows = rows_of(partner(step % N_TIME))
        return pltpu.make_async_copy(volts.at[rows], own.at[rows], load_sem.at[step % N_TIME])

    def start_load(step, carry):
        load(step).start()
        return carry

    def spread(owner, target):
        rows = rows_of(owner)
        for a in range(R):
            wide[a * share : (a + 1) * share, :] = own[rows, a * R : (a + 1) * R].astype(jnp.float32)
        for s in range(share):
            target[s] = wide[pl.ds(s, R, stride=share), :].astype(jnp.bfloat16)

    def send_piece(step, piece):
        owner = partner(step)
        some = pl.ds(piece * per, per)
        pltpu.make_async_remote_copy(
            src_ref=blocks.at[owner, some],
            dst_ref=times.at[tm, some],
            send_sem=send_times,
            recv_sem=recv_times.at[piece],
            device_id={"tm": owner},
            device_id_type=MESH,
        ).start()

    def first_piece(step, carry):
        owner = partner(step)
        load(step).wait()
        spread(owner, blocks.at[owner])
        send_piece(step, 0)
        return carry

    lax.fori_loop(1, N_TIME + 1, start_load, 0)
    sources = (delays_in, dead_in, taps_in, first_in, twist_in, second_in)
    places = (delays, dead_inputs, raw_taps, first, twist, second)
    tables = [
        pltpu.make_async_copy(source, place, table_sem.at[index])
        for index, (source, place) in enumerate(zip(sources, places))
    ]
    for table in tables:
        table.start()
    lax.fori_loop(1, N_TIME, first_piece, 0)

    def later_piece(index, carry):
        send_piece(index % (N_TIME - 1) + 1, index // (N_TIME - 1) + 1)
        return carry

    lax.fori_loop(0, (N_TIME - 1) * (pieces - 1), later_piece, 0)
    load(0).wait()
    spread(tm, times.at[tm])

    for table in tables:
        table.wait()
    for a in range(R):
        taps[pl.ds(a, n_taps, stride=R), :] = raw_taps[:, a * R : (a + 1) * R]
    channels = lax.broadcasted_iota(jnp.int32, (HALF, R), 0) * R + lax.broadcasted_iota(
        jnp.int32, (HALF, R), 1
    )

    def one_rotation(s, carry):
        phases = (two_pi / (R * R)) * (channels * delays[tm * share + s] & (R * R - 1)).astype(jnp.float32)
        weight = (1 - dead_inputs[tm * share + s]).astype(jnp.float32) / R
        rot[0, s] = jnp.cos(phases) * weight
        rot[1, s] = jnp.sin(phases) * weight
        return carry

    lax.fori_loop(0, share, one_rotation, 0)

    low = lax.broadcasted_iota(jnp.int32, (HALF, R), 1) < HALF

    def one_signal(s, carry):
        spectrum = [None] * N_TIME
        for t in range(N_TIME):
            filtered = taps[:R] * times[t, s].astype(jnp.float32)
            for j in range(1, min(n_taps, t + 1)):
                filtered = filtered + taps[j * R : (j + 1) * R] * times[t - j, s].astype(jnp.float32)
            sums = jnp.dot(
                first[...], filtered.astype(jnp.bfloat16), preferred_element_type=jnp.float32
            )
            real, imag = sums[:R], sums[R:]
            turned = jnp.concatenate(
                [
                    (real * twist[0] + imag * twist[1]).astype(jnp.bfloat16),
                    (imag * twist[0] - real * twist[1]).astype(jnp.bfloat16),
                ],
                axis=1,
            )
            raw = lax.dot_general(
                second[...],
                turned,
                (((1,), (1,)), ((), ())),
                preferred_element_type=jnp.float32,
            )
            rot_cos, rot_sin = rot[0, s], rot[1, s]
            spectrum[t] = (
                raw[:HALF] * rot_cos - raw[HALF:] * rot_sin,
                raw[:HALF] * rot_sin + raw[HALF:] * rot_cos,
            )
            if t % 2 == 1:
                for part in range(2):
                    even, odd = spectrum[t - 1][part], spectrum[t][part]
                    lower = jnp.where(low, even, pltpu.roll(odd, HALF, 1))
                    upper = jnp.where(low, pltpu.roll(even, HALF, 1), odd)
                    tile = (t // 2) * 2 + part
                    for half, value in enumerate((lower, upper)):
                        row = ((tile * 2 + half) * share + s) * HALF
                        turned_rows[pl.ds(pl.multiple_of(row, HALF), HALF), :] = value
        return carry

    def one_piece(piece, carry):
        arrived = times.at[pl.ds(0, N_TIME - 1), pl.ds(piece * per, per)]
        pltpu.make_async_copy(arrived, arrived, recv_times.at[piece]).wait()
        lax.fori_loop(piece * per, (piece + 1) * per, one_signal, 0)
        return carry

    lax.fori_loop(0, pieces, one_piece, 0)

    here = pl.ds(pl.multiple_of((chan * N_TIME + tm) * share, share), share)
    x, y, z, core = place()

    def owner_of(step):
        to_x = (x + step // 16 + step) % 4
        to_y = (y + step) % 4
        to_z = (z + step // 4 + step) % 4
        return to_x // 2 * 4 + to_y, to_z * 2 + to_x % 2

    def gather_rows(m, half):
        for tile in range(N_TIME):
            base = (tile * 2 + half) * share * HALF
            rows = turned_rows[pl.ds(base + m, share, stride=HALF), :]
            spectra[2 * m + half, :, tile * R : (tile + 1) * R] = rows.astype(jnp.bfloat16)

    def send_half(step, half):
        to_tm, to_pair = owner_of(step)
        pltpu.make_async_remote_copy(
            src_ref=spectra.at[(to_tm * 8 + to_pair) * 2 + half],
            dst_ref=out.at[here],
            send_sem=send_spectra,
            recv_sem=recv_spectra,
            device_id={"tm": to_tm, "chan": to_pair * 2 + half},
            device_id_type=MESH,
        ).start()

    def one_chip(step, carry):
        to_tm, to_pair = owner_of(step)
        for half in range(2):
            gather_rows(to_tm * 8 + to_pair, half)
        for half in range(2):
            send_half(step, half)
        return carry

    lax.fori_loop(1, groups // 2, one_chip, 0)
    for half in range(2):
        gather_rows(tm * 8 + chan // 2, half)
    send_half(0, 1 - core)
    pltpu.make_async_copy(spectra.at[tm * N_CHAN + chan], out.at[here], recv_spectra).start()

    sent = blocks.at[pl.ds(0, N_TIME - 1)]
    pltpu.make_async_copy(sent, sent, send_times).wait()
    sent = spectra.at[pl.ds(0, groups - 1)]
    pltpu.make_async_copy(sent, sent, send_spectra).wait()
    pltpu.make_async_copy(out, out, recv_spectra).wait()


def correlate_kernel(scale, spectra, out, left, right):
    signals, depth = left.shape
    block = out.shape[1]
    tall = 2 * block
    j = pl.program_id(0)

    @pl.when(j == 0)
    def _():
        left[...] = spectra[...]
        for b in range(signals // block):
            right[b] = spectra[b * block : (b + 1) * block, :].T

    def product(rows):
        sums = jnp.dot(left[rows, :], right[j], preferred_element_type=jnp.float32)
        return (sums * scale).astype(out.dtype)

    for m in range(signals // tall):
        rows = slice(m * tall, (m + 1) * tall)
        out[rows, :] = product(rows)
    here = pl.ds(pl.multiple_of(j * block, block), block)
    own = left[here, :]
    for pair in range(depth // (2 * R)):
        real = slice(2 * pair * R, (2 * pair + 1) * R)
        imag = slice((2 * pair + 1) * R, (2 * pair + 2) * R)
        left[here, real] = own[:, imag]
        left[here, imag] = -own[:, real]
    shape = (block, block)
    lower = lax.broadcasted_iota(jnp.int32, shape, 0) >= lax.broadcasted_iota(jnp.int32, shape, 1)
    out[here, :] = jnp.where(lower, out[here, :], product(here))


def shards(voltages, filter_taps, delays, dead_inputs):
    signals_here = voltages.shape[0]
    share = signals_here // N_TIME
    signals = signals_here * N_CHAN
    groups = N_TIME * N_CHAN
    depth = N_TIME * R
    in_hbm = pl.BlockSpec(memory_space=pltpu.HBM)
    pieces = 8
    tables = dft_tables()

    everyone = pl.pallas_call(
        channel_kernel,
        out_shape=jax.ShapeDtypeStruct((signals, depth), jnp.bfloat16),
        in_specs=[in_hbm] * 7,
        out_specs=in_hbm,
        scratch_shapes=[
            pltpu.SMEM(delays.shape, jnp.int32),
            pltpu.SMEM(dead_inputs.shape, jnp.int32),
            pltpu.VMEM(filter_taps.shape, jnp.float32),
            *(pltpu.VMEM(table.shape, table.dtype) for table in tables),
            pltpu.VMEM(voltages.shape, jnp.bfloat16),
            pltpu.VMEM((R * share, R), jnp.float32),
            pltpu.VMEM((N_TIME, share, R, R), jnp.bfloat16),
            pltpu.VMEM((N_TIME, share, R, R), jnp.bfloat16),
            pltpu.VMEM((filter_taps.shape[0] * R, R), jnp.float32),
            pltpu.VMEM((2, share, HALF, R), jnp.float32),
            pltpu.VMEM((N_TIME * 2 * share * HALF, R), jnp.float32),
            pltpu.VMEM((groups, share, depth), jnp.bfloat16),
            pltpu.SemaphoreType.DMA((3 + len(tables),)),
            pltpu.SemaphoreType.DMA((N_TIME,)),
            pltpu.SemaphoreType.DMA,
            pltpu.SemaphoreType.DMA((pieces,)),
            pltpu.SemaphoreType.DMA,
            pltpu.SemaphoreType.DMA,
        ],
        compiler_params=pltpu.CompilerParams(has_side_effects=True, vmem_limit_bytes=48 * 2**20),
        name="channels",
    )(voltages, delays, dead_inputs, filter_taps, *tables)

    block = 256
    scale = 1.0 / (HALF * N_TIME)
    return pl.pallas_call(
        functools.partial(correlate_kernel, scale),
        grid=(signals // block,),
        out_shape=jax.ShapeDtypeStruct((1, signals, signals), jnp.bfloat16),
        in_specs=[pl.BlockSpec((signals, depth), lambda j: (0, 0), pipeline_mode=pl.Buffered(1))],
        out_specs=pl.BlockSpec((None, signals, block), lambda j: (0, 0, j)),
        scratch_shapes=[
            pltpu.VMEM((signals, depth), jnp.bfloat16),
            pltpu.VMEM((signals // block, depth, block), jnp.bfloat16),
        ],
        compiler_params=pltpu.CompilerParams(vmem_limit_bytes=40 * 2**20),
        name="correlate",
    )(everyone)


def solution(mesh):
    in_specs = (P("chan", "tm"), P(), P("chan"), P("chan"))
    out_specs = P(("tm", "chan"), None, None)
    return jax.shard_map(shards, mesh=mesh, in_specs=in_specs, out_specs=out_specs, check_vma=False)
```

```python
import functools

import jax
import jax.numpy as jnp
import numpy as np
from jax import lax
from jax.experimental import pallas as pl
from jax.experimental.pallas import tpu as pltpu
from jax.sharding import PartitionSpec as P

R = 128
HALF = R // 2
N_TIME = 8
N_CHAN = 16
VMEM_LIMIT = 60 * 2**20
EARLY, LATE = 4, 4
MESH = pl.DeviceIdType.MESH
two_pi = 2.0 * np.pi


def dft_tables():
    indices = np.arange(R)
    outer = indices[:, None] * indices[None, :]
    angles = two_pi / R * (outer % R)
    cos, sin = np.cos(angles), np.sin(angles)
    first = np.concatenate([cos, -sin], axis=0)
    twist = two_pi / (R * R) * outer
    cos_m, sin_m = cos[:HALF], sin[:HALF]
    second = np.concatenate(
        [np.concatenate([cos_m, sin_m], axis=1), np.concatenate([-sin_m, cos_m], axis=1)], axis=0
    )
    return (
        jnp.asarray(first, jnp.bfloat16),
        jnp.asarray(np.stack([np.cos(twist), np.sin(twist)]), jnp.float32),
        jnp.asarray(second, jnp.bfloat16),
    )


def place():
    tm, chan = lax.axis_index("tm"), lax.axis_index("chan")
    return 2 * (tm // 4) + chan // 2 % 2, tm % 4, chan // 4, chan % 2


def channel_kernel(
    scale,
    volts, delays_in, dead_in, taps_in, first_in, twist_in, second_in,
    late, early_sums,
    delays, dead_inputs, raw_taps, first, twist, second,
    own, wide, blocks, times, taps, rot, turned_rows, early_spectra, late_spectra,
    early, right, sums_out,
    table_sem, load_sem, send_times, recv_times, send_spectra, recv_early, recv_late, sums_sem,
):
    share = times.shape[1]
    n_taps = raw_taps.shape[0]
    pieces = recv_times.shape[0]
    per = share // pieces
    groups = early_spectra.shape[0]
    tm, chan = lax.axis_index("tm"), lax.axis_index("chan")

    def partner(step):
        along_y = (3 * step) % 4
        across = step % 2 * (1 - step // 4) + (1 - step % 2) * (step // 4)
        return (tm // 4 + across) % 2 * 4 + (tm + along_y) % 4

    def rows_of(owner):
        return pl.ds(pl.multiple_of(owner * share, share), share)

    def load(step):
        rows = rows_of(partner(step % N_TIME))
        return pltpu.make_async_copy(volts.at[rows], own.at[rows], load_sem.at[step % N_TIME])

    def start_load(step, carry):
        load(step).start()
        return carry

    def spread(owner, target):
        rows = rows_of(owner)
        for a in range(R):
            wide[a * share : (a + 1) * share, :] = own[rows, a * R : (a + 1) * R].astype(jnp.float32)
        for s in range(share):
            target[s] = wide[pl.ds(s, R, stride=share), :].astype(jnp.bfloat16)

    def send_piece(step, piece):
        owner = partner(step)
        some = pl.ds(piece * per, per)
        pltpu.make_async_remote_copy(
            src_ref=blocks.at[owner, some],
            dst_ref=times.at[tm, some],
            send_sem=send_times,
            recv_sem=recv_times.at[piece],
            device_id={"tm": owner},
            device_id_type=MESH,
        ).start()

    def first_piece(step, carry):
        owner = partner(step)
        load(step).wait()
        spread(owner, blocks.at[owner])
        send_piece(step, 0)
        return carry

    lax.fori_loop(1, N_TIME + 1, start_load, 0)
    sources = (delays_in, dead_in, taps_in, first_in, twist_in, second_in)
    places = (delays, dead_inputs, raw_taps, first, twist, second)
    tables = [
        pltpu.make_async_copy(source, place, table_sem.at[index])
        for index, (source, place) in enumerate(zip(sources, places))
    ]
    for table in tables:
        table.start()
    lax.fori_loop(1, N_TIME, first_piece, 0)

    def later_piece(index, carry):
        send_piece(index % (N_TIME - 1) + 1, index // (N_TIME - 1) + 1)
        return carry

    lax.fori_loop(0, (N_TIME - 1) * (pieces - 1), later_piece, 0)
    load(0).wait()
    spread(tm, times.at[tm])

    for table in tables:
        table.wait()
    for a in range(R):
        taps[pl.ds(a, n_taps, stride=R), :] = raw_taps[:, a * R : (a + 1) * R]
    channels = lax.broadcasted_iota(jnp.int32, (HALF, R), 0) * R + lax.broadcasted_iota(
        jnp.int32, (HALF, R), 1
    )

    def one_rotation(s, carry):
        phases = (two_pi / (R * R)) * (channels * delays[tm * share + s] & (R * R - 1)).astype(jnp.float32)
        weight = (1 - dead_inputs[tm * share + s]).astype(jnp.float32) / R
        rot[0, s] = jnp.cos(phases) * weight
        rot[1, s] = jnp.sin(phases) * weight
        return carry

    lax.fori_loop(0, share, one_rotation, 0)

    low = lax.broadcasted_iota(jnp.int32, (HALF, R), 1) < HALF

    def one_signal(s, carry):
        spectrum = [None] * N_TIME
        for t in range(N_TIME):
            filtered = taps[:R] * times[t, s].astype(jnp.float32)
            for j in range(1, min(n_taps, t + 1)):
                filtered = filtered + taps[j * R : (j + 1) * R] * times[t - j, s].astype(jnp.float32)
            sums = jnp.dot(
                first[...], filtered.astype(jnp.bfloat16), preferred_element_type=jnp.float32
            )
            real, imag = sums[:R], sums[R:]
            turned = jnp.concatenate(
                [
                    (real * twist[0] + imag * twist[1]).astype(jnp.bfloat16),
                    (imag * twist[0] - real * twist[1]).astype(jnp.bfloat16),
                ],
                axis=1,
            )
            raw = lax.dot_general(
                second[...],
                turned,
                (((1,), (1,)), ((), ())),
                preferred_element_type=jnp.float32,
            )
            rot_cos, rot_sin = rot[0, s], rot[1, s]
            spectrum[t] = (
                raw[:HALF] * rot_cos - raw[HALF:] * rot_sin,
                raw[:HALF] * rot_sin + raw[HALF:] * rot_cos,
            )
            if t % 2 == 1:
                for part in range(2):
                    even, odd = spectrum[t - 1][part], spectrum[t][part]
                    lower = jnp.where(low, even, pltpu.roll(odd, HALF, 1))
                    upper = jnp.where(low, pltpu.roll(even, HALF, 1), odd)
                    tile = (t // 2) * 2 + part
                    for half, value in enumerate((lower, upper)):
                        row = ((tile * 2 + half) * share + s) * HALF
                        turned_rows[pl.ds(pl.multiple_of(row, HALF), HALF), :] = value
        return carry

    def one_piece(piece, carry):
        arrived = times.at[pl.ds(0, N_TIME - 1), pl.ds(piece * per, per)]
        pltpu.make_async_copy(arrived, arrived, recv_times.at[piece]).wait()
        lax.fori_loop(piece * per, (piece + 1) * per, one_signal, 0)
        return carry

    lax.fori_loop(0, pieces, one_piece, 0)

    here = pl.ds(pl.multiple_of((chan * N_TIME + tm) * share, share), share)
    x, y, z, core = place()

    def owner_of(step):
        to_x = (x + step // 16 + step) % 4
        to_y = (y + step) % 4
        to_z = (z + step // 4 + step) % 4
        return to_x // 2 * 4 + to_y, to_z * 2 + to_x % 2

    sources = (early_spectra, late_spectra)

    def gather_rows(m, half, part):
        for index in range((EARLY, LATE)[part]):
            base = ((part * EARLY + index) * 2 + half) * share * HALF
            rows = turned_rows[pl.ds(base + m, share, stride=HALF), :]
            sources[part][2 * m + half, :, index * R : (index + 1) * R] = rows.astype(jnp.bfloat16)

    def send_half(step, half, part):
        to_tm, to_pair = owner_of(step)
        pltpu.make_async_remote_copy(
            src_ref=sources[part].at[(to_tm * 8 + to_pair) * 2 + half],
            dst_ref=(early, late)[part].at[here],
            send_sem=send_spectra.at[part],
            recv_sem=(recv_early, recv_late)[part],
            device_id={"tm": to_tm, "chan": to_pair * 2 + half},
            device_id_type=MESH,
        ).start()

    for part in range(2):

        def one_chip(step, carry):
            to_tm, to_pair = owner_of(step)
            for half in range(2):
                gather_rows(to_tm * 8 + to_pair, half, part)
            for half in range(2):
                send_half(step, half, part)
            return carry

        lax.fori_loop(1, groups // 2, one_chip, 0)
        for half in range(2):
            gather_rows(tm * 8 + chan // 2, half, part)
        send_half(0, 1 - core, part)
        pltpu.make_async_copy(
            sources[part].at[tm * N_CHAN + chan], (early, late)[part].at[here], (recv_early, recv_late)[part]
        ).start()

    pltpu.make_async_copy(early, early, recv_early).wait()
    block = right.shape[1]

    def sums_copy(j):
        columns = pl.ds(pl.multiple_of(j * block, block), block)
        return pltpu.make_async_copy(sums_out.at[j % 2], early_sums.at[:, columns], sums_sem.at[j % 2])

    def column(j, carry):
        @pl.when(j >= 2)
        def _():
            sums_copy(j - 2).wait()

        def emit(rows, sums, lower):
            total = (sums * scale).astype(jnp.bfloat16)
            slot = sums_out.at[j % 2]
            slot[rows, :] = total if lower is None else jnp.where(lower, slot[rows, :], total)

        column_block(early, right, j, emit)
        sums_copy(j).start()
        return carry

    columns = early_sums.shape[1] // block
    lax.fori_loop(0, columns, column, 0)
    sums_copy(columns - 2).wait()
    sums_copy(columns - 1).wait()

    sent = blocks.at[pl.ds(0, N_TIME - 1)]
    pltpu.make_async_copy(sent, sent, send_times).wait()
    for part in range(2):
        sent = sources[part].at[pl.ds(0, groups - 1)]
        pltpu.make_async_copy(sent, sent, send_spectra.at[part]).wait()
    pltpu.make_async_copy(late, late, recv_late).wait()


def column_block(left, right, j, emit):
    signals, depth = left.shape
    block = right.shape[1]
    tall = signals
    here = pl.ds(pl.multiple_of(j * block, block), block)
    right[...] = left[here, :].T

    def product(rows):
        return jnp.dot(left[rows, :], right[...], preferred_element_type=jnp.float32)

    for m in range(signals // tall):
        rows = pl.ds(m * tall, tall)
        emit(rows, product(rows), None)
    own = left[here, :]
    for pair in range(depth // (2 * R)):
        real = slice(2 * pair * R, (2 * pair + 1) * R)
        imag = slice((2 * pair + 1) * R, (2 * pair + 2) * R)
        left[here, real] = own[:, imag]
        left[here, imag] = -own[:, real]
    shape = (block, block)
    lower = lax.broadcasted_iota(jnp.int32, shape, 0) >= lax.broadcasted_iota(jnp.int32, shape, 1)
    emit(here, product(here), lower)


def correlate_kernel(scale, late, early_sums, out, left, right, sums_in, result, late_sem, in_sem, out_sem):
    block = right.shape[1]
    columns = out.shape[2] // block

    def columns_of(j):
        return pl.ds(pl.multiple_of(j * block, block), block)

    def load(j):
        return pltpu.make_async_copy(early_sums.at[:, columns_of(j)], sums_in.at[j], in_sem.at[j])

    def store(j):
        return pltpu.make_async_copy(result.at[j], out.at[0, :, columns_of(j)], out_sem.at[j])

    load_left = pltpu.make_async_copy(late, left, late_sem)
    load_left.start()
    for j in range(columns):
        load(j).start()
    load_left.wait()

    def column(j, carry):
        load(j).wait()
        earlier, total = sums_in.at[j], result.at[j]

        def emit(rows, sums, lower):
            values = (sums * scale + earlier[rows, :].astype(jnp.float32)).astype(out.dtype)
            total[rows, :] = values if lower is None else jnp.where(lower, total[rows, :], values)

        column_block(left, right, j, emit)
        store(j).start()
        return carry

    lax.fori_loop(0, columns, column, 0)
    for j in range(columns):
        store(j).wait()


def shards(voltages, filter_taps, delays, dead_inputs):
    signals_here = voltages.shape[0]
    share = signals_here // N_TIME
    signals = signals_here * N_CHAN
    groups = N_TIME * N_CHAN
    in_hbm = pl.BlockSpec(memory_space=pltpu.HBM)
    pieces = 16
    block, last_block = 512, 512
    scale = 1.0 / (HALF * N_TIME)
    tables = dft_tables()

    late, early_sums = pl.pallas_call(
        functools.partial(channel_kernel, scale),
        out_shape=[
            jax.ShapeDtypeStruct((signals, LATE * R), jnp.bfloat16),
            jax.ShapeDtypeStruct((signals, signals), jnp.bfloat16),
        ],
        in_specs=[in_hbm] * 7,
        out_specs=[in_hbm, in_hbm],
        scratch_shapes=[
            pltpu.SMEM(delays.shape, jnp.int32),
            pltpu.SMEM(dead_inputs.shape, jnp.int32),
            pltpu.VMEM(filter_taps.shape, jnp.float32),
            *(pltpu.VMEM(table.shape, table.dtype) for table in tables),
            pltpu.VMEM(voltages.shape, jnp.bfloat16),
            pltpu.VMEM((R * share, R), jnp.float32),
            pltpu.VMEM((N_TIME, share, R, R), jnp.bfloat16),
            pltpu.VMEM((N_TIME, share, R, R), jnp.bfloat16),
            pltpu.VMEM((filter_taps.shape[0] * R, R), jnp.float32),
            pltpu.VMEM((2, share, HALF, R), jnp.float32),
            pltpu.VMEM((N_TIME * 2 * share * HALF, R), jnp.float32),
            pltpu.VMEM((groups, share, EARLY * R), jnp.bfloat16),
            pltpu.VMEM((groups, share, LATE * R), jnp.bfloat16),
            pltpu.VMEM((signals, EARLY * R), jnp.bfloat16),
            pltpu.VMEM((EARLY * R, block), jnp.bfloat16),
            pltpu.VMEM((2, signals, block), jnp.bfloat16),
            pltpu.SemaphoreType.DMA((3 + len(tables),)),
            pltpu.SemaphoreType.DMA((N_TIME,)),
            pltpu.SemaphoreType.DMA,
            pltpu.SemaphoreType.DMA((pieces,)),
            pltpu.SemaphoreType.DMA((2,)),
            pltpu.SemaphoreType.DMA,
            pltpu.SemaphoreType.DMA,
            pltpu.SemaphoreType.DMA((2,)),
        ],
        compiler_params=pltpu.CompilerParams(has_side_effects=True, vmem_limit_bytes=VMEM_LIMIT),
        name="channels",
    )(voltages, delays, dead_inputs, filter_taps, *tables)

    return pl.pallas_call(
        functools.partial(correlate_kernel, scale),
        out_shape=jax.ShapeDtypeStruct((1, signals, signals), jnp.bfloat16),
        in_specs=[in_hbm, in_hbm],
        out_specs=in_hbm,
        scratch_shapes=[
            pltpu.VMEM((signals, LATE * R), jnp.bfloat16),
            pltpu.VMEM((LATE * R, last_block), jnp.bfloat16),
            pltpu.VMEM((signals // last_block, signals, last_block), jnp.bfloat16),
            pltpu.VMEM((signals // last_block, signals, last_block), jnp.bfloat16),
            pltpu.SemaphoreType.DMA,
            pltpu.SemaphoreType.DMA((signals // last_block,)),
            pltpu.SemaphoreType.DMA((signals // last_block,)),
        ],
        compiler_params=pltpu.CompilerParams(vmem_limit_bytes=VMEM_LIMIT),
        name="correlate",
    )(late, early_sums)


def solution(mesh):
    in_specs = (P("chan", "tm"), P(), P("chan"), P("chan"))
    out_specs = P(("tm", "chan"), None, None)
    return jax.shard_map(shards, mesh=mesh, in_specs=in_specs, out_specs=out_specs, check_vma=False)
```

```python
import functools

import jax
import jax.numpy as jnp
import numpy as np
from jax import lax
from jax.experimental import pallas as pl
from jax.experimental.pallas import tpu as pltpu
from jax.sharding import PartitionSpec as P

R = 128
HALF = R // 2
N_TIME = 8
N_CHAN = 16
VMEM_LIMIT = 60 * 2**20
PARTS = (4, 2, 2)
MESH = pl.DeviceIdType.MESH
two_pi = 2.0 * np.pi


def dft_tables():
    indices = np.arange(R)
    outer = indices[:, None] * indices[None, :]
    angles = two_pi / R * (outer % R)
    cos, sin = np.cos(angles), np.sin(angles)
    first = np.concatenate([cos, -sin], axis=0)
    twist = two_pi / (R * R) * outer
    cos_m, sin_m = cos[:HALF], sin[:HALF]
    second = np.concatenate(
        [np.concatenate([cos_m, sin_m], axis=1), np.concatenate([-sin_m, cos_m], axis=1)], axis=0
    )
    return (
        jnp.asarray(first, jnp.bfloat16),
        jnp.asarray(np.stack([np.cos(twist), np.sin(twist)]), jnp.float32),
        jnp.asarray(second, jnp.bfloat16),
    )


def place():
    tm, chan = lax.axis_index("tm"), lax.axis_index("chan")
    return 2 * (tm // 4) + chan // 2 % 2, tm % 4, chan // 4, chan % 2


def channel_kernel(
    scale,
    volts, delays_in, dead_in, taps_in, first_in, twist_in, second_in,
    late, early_sums,
    delays, dead_inputs, raw_taps, first, twist, second,
    own, wide, blocks, times, taps, rot, turned_rows, outgoing,
    earlies, rights, early_total, sums_out,
    table_sem, load_sem, send_times, recv_times, send_spectra, recv_spectra, sums_sem, everyone_in,
):
    share = times.shape[1]
    n_taps = raw_taps.shape[0]
    pieces = recv_times.shape[0]
    per = share // pieces
    groups = outgoing[0].shape[0]
    tm, chan = lax.axis_index("tm"), lax.axis_index("chan")

    barrier = pltpu.get_barrier_semaphore()

    def greet(sem, axis, size):
        def one(step, carry):
            other = lax.rem(lax.axis_index(axis) + step, size)
            pl.semaphore_signal(sem, inc=1, device_id={axis: other}, device_id_type=MESH)
            return carry

        lax.fori_loop(1, size, one, 0)

    greet(barrier, "tm", N_TIME)
    greet(barrier, "chan", N_CHAN)

    def partner(step):
        along_y = (3 * step) % 4
        across = step % 2 * (1 - step // 4) + (1 - step % 2) * (step // 4)
        return (tm // 4 + across) % 2 * 4 + (tm + along_y) % 4

    def rows_of(owner):
        return pl.ds(pl.multiple_of(owner * share, share), share)

    def load(step):
        rows = rows_of(partner(step % N_TIME))
        return pltpu.make_async_copy(volts.at[rows], own.at[rows], load_sem.at[step % N_TIME])

    def start_load(step, carry):
        load(step).start()
        return carry

    def spread(owner, target):
        rows = rows_of(owner)
        for a in range(R):
            wide[a * share : (a + 1) * share, :] = own[rows, a * R : (a + 1) * R].astype(jnp.float32)
        for s in range(share):
            target[s] = wide[pl.ds(s, R, stride=share), :].astype(jnp.bfloat16)

    def send_piece(step, piece):
        owner = partner(step)
        some = pl.ds(piece * per, per)
        pltpu.make_async_remote_copy(
            src_ref=blocks.at[owner, some],
            dst_ref=times.at[tm, some],
            send_sem=send_times,
            recv_sem=recv_times.at[piece],
            device_id={"tm": owner},
            device_id_type=MESH,
        ).start()

    def first_piece(step, carry):
        owner = partner(step)
        load(step).wait()
        spread(owner, blocks.at[owner])

        @pl.when(step == 1)
        def _():
            pl.semaphore_wait(barrier, N_TIME - 1 + N_CHAN - 1)
            greet(everyone_in, "tm", N_TIME)

        send_piece(step, 0)
        return carry

    lax.fori_loop(1, N_TIME + 1, start_load, 0)
    sources = (delays_in, dead_in, taps_in, first_in, twist_in, second_in)
    places = (delays, dead_inputs, raw_taps, first, twist, second)
    tables = [
        pltpu.make_async_copy(source, place, table_sem.at[index])
        for index, (source, place) in enumerate(zip(sources, places))
    ]
    for table in tables:
        table.start()
    lax.fori_loop(1, N_TIME, first_piece, 0)

    def later_piece(index, carry):
        send_piece(index % (N_TIME - 1) + 1, index // (N_TIME - 1) + 1)
        return carry

    lax.fori_loop(0, (N_TIME - 1) * (pieces - 1), later_piece, 0)
    load(0).wait()
    spread(tm, times.at[tm])

    for table in tables:
        table.wait()
    for a in range(R):
        taps[pl.ds(a, n_taps, stride=R), :] = raw_taps[:, a * R : (a + 1) * R]
    channels = lax.broadcasted_iota(jnp.int32, (HALF, R), 0) * R + lax.broadcasted_iota(
        jnp.int32, (HALF, R), 1
    )

    def one_rotation(s, carry):
        phases = (two_pi / (R * R)) * (channels * delays[tm * share + s] & (R * R - 1)).astype(jnp.float32)
        weight = (1 - dead_inputs[tm * share + s]).astype(jnp.float32) / R
        rot[0, s] = jnp.cos(phases) * weight
        rot[1, s] = jnp.sin(phases) * weight
        return carry

    lax.fori_loop(0, share, one_rotation, 0)

    low = lax.broadcasted_iota(jnp.int32, (HALF, R), 1) < HALF

    def one_signal(s, carry):
        spectrum = [None] * N_TIME
        for t in range(N_TIME):
            filtered = taps[:R] * times[t, s].astype(jnp.float32)
            for j in range(1, min(n_taps, t + 1)):
                filtered = filtered + taps[j * R : (j + 1) * R] * times[t - j, s].astype(jnp.float32)
            sums = jnp.dot(
                first[...], filtered.astype(jnp.bfloat16), preferred_element_type=jnp.float32
            )
            real, imag = sums[:R], sums[R:]
            turned = jnp.concatenate(
                [
                    (real * twist[0] + imag * twist[1]).astype(jnp.bfloat16),
                    (imag * twist[0] - real * twist[1]).astype(jnp.bfloat16),
                ],
                axis=1,
            )
            raw = lax.dot_general(
                second[...],
                turned,
                (((1,), (1,)), ((), ())),
                preferred_element_type=jnp.float32,
            )
            rot_cos, rot_sin = rot[0, s], rot[1, s]
            spectrum[t] = (
                raw[:HALF] * rot_cos - raw[HALF:] * rot_sin,
                raw[:HALF] * rot_sin + raw[HALF:] * rot_cos,
            )
            if t % 2 == 1:
                for part in range(2):
                    even, odd = spectrum[t - 1][part], spectrum[t][part]
                    lower = jnp.where(low, even, pltpu.roll(odd, HALF, 1))
                    upper = jnp.where(low, pltpu.roll(even, HALF, 1), odd)
                    tile = (t // 2) * 2 + part
                    for half, value in enumerate((lower, upper)):
                        row = ((tile * 2 + half) * share + s) * HALF
                        turned_rows[pl.ds(pl.multiple_of(row, HALF), HALF), :] = value
        return carry

    def one_piece(piece, carry):
        arrived = times.at[pl.ds(0, N_TIME - 1), pl.ds(piece * per, per)]
        pltpu.make_async_copy(arrived, arrived, recv_times.at[piece]).wait()
        lax.fori_loop(piece * per, (piece + 1) * per, one_signal, 0)
        return carry

    lax.fori_loop(0, pieces, one_piece, 0)

    here = pl.ds(pl.multiple_of((chan * N_TIME + tm) * share, share), share)
    x, y, z, core = place()

    def owner_of(step):
        to_x = (x + step // 16 + step) % 4
        to_y = (y + step) % 4
        to_z = (z + step // 4 + step) % 4
        return to_x // 2 * 4 + to_y, to_z * 2 + to_x % 2

    received = (*earlies, late)

    def gather_rows(m, half, part):
        for index in range(PARTS[part]):
            base = ((sum(PARTS[:part]) + index) * 2 + half) * share * HALF
            rows = turned_rows[pl.ds(base + m, share, stride=HALF), :]
            outgoing[part][2 * m + half, :, index * R : (index + 1) * R] = rows.astype(jnp.bfloat16)

    def send_half(step, half, part):
        to_tm, to_pair = owner_of(step)
        pltpu.make_async_remote_copy(
            src_ref=outgoing[part].at[(to_tm * 8 + to_pair) * 2 + half],
            dst_ref=received[part].at[here],
            send_sem=send_spectra.at[part],
            recv_sem=recv_spectra.at[part],
            device_id={"tm": to_tm, "chan": to_pair * 2 + half},
            device_id_type=MESH,
        ).start()

    pl.semaphore_wait(everyone_in, N_TIME - 1)
    for part in range(len(PARTS)):

        def one_chip(step, carry):
            to_tm, to_pair = owner_of(step)
            for half in range(2):
                gather_rows(to_tm * 8 + to_pair, half, part)
            for half in range(2):
                send_half(step, half, part)
            return carry

        lax.fori_loop(1, groups // 2, one_chip, 0)
        for half in range(2):
            gather_rows(tm * 8 + chan // 2, half, part)
        send_half(0, 1 - core, part)
        pltpu.make_async_copy(
            outgoing[part].at[tm * N_CHAN + chan], received[part].at[here], recv_spectra.at[part]
        ).start()

    def arrive(part):
        pltpu.make_async_copy(received[part], received[part], recv_spectra.at[part]).wait()

    block = sums_out.shape[2]
    columns = early_sums.shape[1] // block

    def first_column(j, carry):
        total = early_total.at[j]

        def emit(rows, sums, lower):
            total[rows, :] = sums if lower is None else jnp.where(lower, total[rows, :], sums)

        column_block(earlies[0], rights[0], j, emit)
        return carry

    def sums_copy(j):
        some = pl.ds(pl.multiple_of(j * block, block), block)
        return pltpu.make_async_copy(sums_out.at[j % 2], early_sums.at[:, some], sums_sem.at[j % 2])

    def second_column(j, carry):
        @pl.when(j >= 2)
        def _():
            sums_copy(j - 2).wait()

        def emit(rows, sums, lower):
            slot = sums_out.at[j % 2]
            total = ((early_total[j, rows, :] + sums) * scale).astype(jnp.bfloat16)
            slot[rows, :] = total if lower is None else jnp.where(lower, slot[rows, :], total)

        column_block(earlies[1], rights[1], j, emit)
        sums_copy(j).start()
        return carry

    arrive(0)
    lax.fori_loop(0, columns, first_column, 0)
    arrive(1)
    lax.fori_loop(0, columns, second_column, 0)
    sums_copy(columns - 2).wait()
    sums_copy(columns - 1).wait()

    sent = blocks.at[pl.ds(0, N_TIME - 1)]
    pltpu.make_async_copy(sent, sent, send_times).wait()
    for part in range(len(PARTS)):
        sent = outgoing[part].at[pl.ds(0, groups - 1)]
        pltpu.make_async_copy(sent, sent, send_spectra.at[part]).wait()
    arrive(len(PARTS) - 1)


def column_block(left, right, j, emit):
    signals, depth = left.shape
    block = right.shape[1]
    tall = signals
    here = pl.ds(pl.multiple_of(j * block, block), block)
    right[...] = left[here, :].T

    def product(rows):
        return jnp.dot(left[rows, :], right[...], preferred_element_type=jnp.float32)

    for m in range(signals // tall):
        rows = pl.ds(m * tall, tall)
        emit(rows, product(rows), None)
    own = left[here, :]
    for pair in range(depth // (2 * R)):
        real = slice(2 * pair * R, (2 * pair + 1) * R)
        imag = slice((2 * pair + 1) * R, (2 * pair + 2) * R)
        left[here, real] = own[:, imag]
        left[here, imag] = -own[:, real]
    shape = (block, block)
    lower = lax.broadcasted_iota(jnp.int32, shape, 0) >= lax.broadcasted_iota(jnp.int32, shape, 1)
    emit(here, product(here), lower)


def correlate_kernel(scale, late, early_sums, out, left, right, sums_in, result, late_sem, in_sem, out_sem):
    block = right.shape[1]
    columns = out.shape[2] // block

    def columns_of(j):
        return pl.ds(pl.multiple_of(j * block, block), block)

    def load(j):
        return pltpu.make_async_copy(early_sums.at[:, columns_of(j)], sums_in.at[j], in_sem.at[j])

    def store(j):
        return pltpu.make_async_copy(result.at[j], out.at[0, :, columns_of(j)], out_sem.at[j])

    load_left = pltpu.make_async_copy(late, left, late_sem)
    load_left.start()
    for j in range(columns):
        load(j).start()
    load_left.wait()

    def column(j, carry):
        load(j).wait()
        earlier, total = sums_in.at[j], result.at[j]

        def emit(rows, sums, lower):
            values = (sums * scale + earlier[rows, :].astype(jnp.float32)).astype(out.dtype)
            total[rows, :] = values if lower is None else jnp.where(lower, total[rows, :], values)

        column_block(left, right, j, emit)
        store(j).start()
        return carry

    lax.fori_loop(0, columns, column, 0)
    for j in range(columns):
        store(j).wait()


def shards(voltages, filter_taps, delays, dead_inputs):
    signals_here = voltages.shape[0]
    share = signals_here // N_TIME
    signals = signals_here * N_CHAN
    groups = N_TIME * N_CHAN
    in_hbm = pl.BlockSpec(memory_space=pltpu.HBM)
    pieces = 16
    block, last_block = 512, 512
    scale = 1.0 / (HALF * N_TIME)
    tables = dft_tables()

    late, early_sums = pl.pallas_call(
        functools.partial(channel_kernel, scale),
        out_shape=[
            jax.ShapeDtypeStruct((signals, PARTS[-1] * R), jnp.bfloat16),
            jax.ShapeDtypeStruct((signals, signals), jnp.bfloat16),
        ],
        in_specs=[in_hbm] * 7,
        out_specs=[in_hbm, in_hbm],
        scratch_shapes=[
            pltpu.SMEM(delays.shape, jnp.int32),
            pltpu.SMEM(dead_inputs.shape, jnp.int32),
            pltpu.VMEM(filter_taps.shape, jnp.float32),
            *(pltpu.VMEM(table.shape, table.dtype) for table in tables),
            pltpu.VMEM(voltages.shape, jnp.bfloat16),
            pltpu.VMEM((R * share, R), jnp.float32),
            pltpu.VMEM((N_TIME, share, R, R), jnp.bfloat16),
            pltpu.VMEM((N_TIME, share, R, R), jnp.bfloat16),
            pltpu.VMEM((filter_taps.shape[0] * R, R), jnp.float32),
            pltpu.VMEM((2, share, HALF, R), jnp.float32),
            pltpu.VMEM((N_TIME * 2 * share * HALF, R), jnp.float32),
            [pltpu.VMEM((groups, share, part * R), jnp.bfloat16) for part in PARTS],
            [pltpu.VMEM((signals, part * R), jnp.bfloat16) for part in PARTS[:2]],
            [pltpu.VMEM((part * R, block), jnp.bfloat16) for part in PARTS[:2]],
            pltpu.VMEM((signals // block, signals, block), jnp.float32),
            pltpu.VMEM((2, signals, block), jnp.bfloat16),
            pltpu.SemaphoreType.DMA((3 + len(tables),)),
            pltpu.SemaphoreType.DMA((N_TIME,)),
            pltpu.SemaphoreType.DMA,
            pltpu.SemaphoreType.DMA((pieces,)),
            pltpu.SemaphoreType.DMA((len(PARTS),)),
            pltpu.SemaphoreType.DMA((len(PARTS),)),
            pltpu.SemaphoreType.DMA((2,)),
            pltpu.SemaphoreType.REGULAR,
        ],
        compiler_params=pltpu.CompilerParams(collective_id=0, has_side_effects=True, vmem_limit_bytes=VMEM_LIMIT),
        name="channels",
    )(voltages, delays, dead_inputs, filter_taps, *tables)

    return pl.pallas_call(
        functools.partial(correlate_kernel, scale),
        out_shape=jax.ShapeDtypeStruct((1, signals, signals), jnp.bfloat16),
        in_specs=[in_hbm, in_hbm],
        out_specs=in_hbm,
        scratch_shapes=[
            pltpu.VMEM((signals, PARTS[-1] * R), jnp.bfloat16),
            pltpu.VMEM((PARTS[-1] * R, last_block), jnp.bfloat16),
            pltpu.VMEM((signals // last_block, signals, last_block), jnp.bfloat16),
            pltpu.VMEM((signals // last_block, signals, last_block), jnp.bfloat16),
            pltpu.SemaphoreType.DMA,
            pltpu.SemaphoreType.DMA((signals // last_block,)),
            pltpu.SemaphoreType.DMA((signals // last_block,)),
        ],
        compiler_params=pltpu.CompilerParams(vmem_limit_bytes=VMEM_LIMIT),
        name="correlate",
    )(late, early_sums)


def solution(mesh):
    in_specs = (P("chan", "tm"), P(), P("chan"), P("chan"))
    out_specs = P(("tm", "chan"), None, None)
    return jax.shard_map(shards, mesh=mesh, in_specs=in_specs, out_specs=out_specs, check_vma=False)
```

```python
import functools

import jax
import jax.numpy as jnp
import numpy as np
from jax import lax
from jax.experimental import pallas as pl
from jax.experimental.pallas import tpu as pltpu
from jax.sharding import PartitionSpec as P

R = 128
HALF = R // 2
N_TIME = 8
N_CHAN = 16
VMEM_LIMIT = 60 * 2**20
N_PARTS = 4
MESH = pl.DeviceIdType.MESH
two_pi = 2.0 * np.pi


def dft_tables():
    indices = np.arange(R)
    outer = indices[:, None] * indices[None, :]
    angles = two_pi / R * (outer % R)
    cos, sin = np.cos(angles), np.sin(angles)
    first = np.concatenate([cos, -sin], axis=0)
    twist = two_pi / (R * R) * outer
    cos_m, sin_m = cos[:HALF], sin[:HALF]
    second = np.concatenate(
        [np.concatenate([cos_m, sin_m], axis=1), np.concatenate([-sin_m, cos_m], axis=1)], axis=0
    )
    return (
        jnp.asarray(first, jnp.bfloat16),
        jnp.asarray(np.stack([np.cos(twist), np.sin(twist)]), jnp.float32),
        jnp.asarray(second, jnp.bfloat16),
    )


def place():
    tm, chan = lax.axis_index("tm"), lax.axis_index("chan")
    return 2 * (tm // 4) + chan // 2 % 2, tm % 4, chan // 4, chan % 2


def channel_kernel(
    scale,
    volts, delays_in, dead_in, taps_in, first_in, twist_in, second_in,
    late, early_sums,
    delays, dead_inputs, raw_taps, first, twist, second,
    own, wide, blocks, times, taps, rot, turned_rows, outgoing,
    earlies, joined, rights, early_total, sums_out,
    table_sem, load_sem, send_times, recv_times, send_spectra, recv_spectra, sums_sem, everyone_in,
):
    share = times.shape[1]
    n_taps = raw_taps.shape[0]
    pieces = recv_times.shape[0]
    per = share // pieces
    groups = outgoing[0].shape[0]
    tm, chan = lax.axis_index("tm"), lax.axis_index("chan")

    barrier = pltpu.get_barrier_semaphore()

    def greet(sem, axis, size):
        def one(step, carry):
            other = lax.rem(lax.axis_index(axis) + step, size)
            pl.semaphore_signal(sem, inc=1, device_id={axis: other}, device_id_type=MESH)
            return carry

        lax.fori_loop(1, size, one, 0)

    def partner(step):
        along_y = (3 * step) % 4
        across = step % 2 * (1 - step // 4) + (1 - step % 2) * (step // 4)
        return (tm // 4 + across) % 2 * 4 + (tm + along_y) % 4

    def rows_of(owner):
        return pl.ds(pl.multiple_of(owner * share, share), share)

    def load(step):
        rows = rows_of(partner(step % N_TIME))
        return pltpu.make_async_copy(volts.at[rows], own.at[rows], load_sem.at[step % N_TIME])

    def start_load(step, carry):
        load(step).start()
        return carry

    def spread(owner, target):
        rows = rows_of(owner)
        for a in range(R):
            wide[a * share : (a + 1) * share, :] = own[rows, a * R : (a + 1) * R].astype(jnp.float32)
        for s in range(share):
            target[s] = wide[pl.ds(s, R, stride=share), :].astype(jnp.bfloat16)

    def send_piece(step, piece):
        owner = partner(step)
        some = pl.ds(piece * per, per)
        pltpu.make_async_remote_copy(
            src_ref=blocks.at[owner, some],
            dst_ref=times.at[tm, some],
            send_sem=send_times,
            recv_sem=recv_times.at[piece],
            device_id={"tm": owner},
            device_id_type=MESH,
        ).start()

    def first_piece(step, carry):
        owner = partner(step)
        load(step).wait()
        spread(owner, blocks.at[owner])

        @pl.when(step == 1)
        def _():
            pl.semaphore_wait(barrier, N_TIME - 1 + N_CHAN - 1)

        send_piece(step, 0)
        return carry

    lax.fori_loop(1, N_TIME + 1, start_load, 0)
    greet(barrier, "tm", N_TIME)
    greet(barrier, "chan", N_CHAN)
    sources = (delays_in, dead_in, taps_in, first_in, twist_in, second_in)
    places = (delays, dead_inputs, raw_taps, first, twist, second)
    tables = [
        pltpu.make_async_copy(source, place, table_sem.at[index])
        for index, (source, place) in enumerate(zip(sources, places))
    ]
    for table in tables:
        table.start()
    lax.fori_loop(1, N_TIME, first_piece, 0)

    def later_piece(index, carry):
        send_piece(index % (N_TIME - 1) + 1, index // (N_TIME - 1) + 1)
        return carry

    lax.fori_loop(0, (N_TIME - 1) * (pieces - 1), later_piece, 0)

    greet(everyone_in, "tm", N_TIME)
    load(0).wait()
    spread(tm, times.at[tm])

    for table in tables:
        table.wait()
    for a in range(R):
        taps[pl.ds(a, n_taps, stride=R), :] = raw_taps[:, a * R : (a + 1) * R]
    channels = lax.broadcasted_iota(jnp.int32, (HALF, R), 0) * R + lax.broadcasted_iota(
        jnp.int32, (HALF, R), 1
    )

    def one_rotation(s, carry):
        phases = (two_pi / (R * R)) * (channels * delays[tm * share + s] & (R * R - 1)).astype(jnp.float32)
        weight = (1 - dead_inputs[tm * share + s]).astype(jnp.float32) / R
        rot[0, s] = jnp.cos(phases) * weight
        rot[1, s] = jnp.sin(phases) * weight
        return carry

    lax.fori_loop(0, share, one_rotation, 0)

    low = lax.broadcasted_iota(jnp.int32, (HALF, R), 1) < HALF

    def one_signal(s, carry):
        spectrum = [None] * N_TIME
        for t in range(N_TIME):
            filtered = taps[:R] * times[t, s].astype(jnp.float32)
            for j in range(1, min(n_taps, t + 1)):
                filtered = filtered + taps[j * R : (j + 1) * R] * times[t - j, s].astype(jnp.float32)
            sums = jnp.dot(
                first[...], filtered.astype(jnp.bfloat16), preferred_element_type=jnp.float32
            )
            real, imag = sums[:R], sums[R:]
            turned = jnp.concatenate(
                [
                    (real * twist[0] + imag * twist[1]).astype(jnp.bfloat16),
                    (imag * twist[0] - real * twist[1]).astype(jnp.bfloat16),
                ],
                axis=1,
            )
            raw = lax.dot_general(
                second[...],
                turned,
                (((1,), (1,)), ((), ())),
                preferred_element_type=jnp.float32,
            )
            rot_cos, rot_sin = rot[0, s], rot[1, s]
            spectrum[t] = (
                raw[:HALF] * rot_cos - raw[HALF:] * rot_sin,
                raw[:HALF] * rot_sin + raw[HALF:] * rot_cos,
            )
            if t % 2 == 1:
                for part in range(2):
                    even, odd = spectrum[t - 1][part], spectrum[t][part]
                    lower = jnp.where(low, even, pltpu.roll(odd, HALF, 1))
                    upper = jnp.where(low, pltpu.roll(even, HALF, 1), odd)
                    tile = (t // 2) * 2 + part
                    for half, value in enumerate((lower, upper)):
                        row = ((tile * 2 + half) * share + s) * HALF
                        turned_rows[pl.ds(pl.multiple_of(row, HALF), HALF), :] = value
        return carry

    def one_piece(piece, carry):
        arrived = times.at[pl.ds(0, N_TIME - 1), pl.ds(piece * per, per)]
        pltpu.make_async_copy(arrived, arrived, recv_times.at[piece]).wait()
        lax.fori_loop(piece * per, (piece + 1) * per, one_signal, 0)
        return carry

    here = pl.ds(pl.multiple_of((chan * N_TIME + tm) * share, share), share)
    x, y, z, core = place()

    def owner_of(step):
        to_x = (x + step // 16 + step) % 4
        to_y = (y + step) % 4
        to_z = (z + step // 4 + step) % 4
        return to_x // 2 * 4 + to_y, to_z * 2 + to_x % 2

    received = (*earlies, late)
    few = share // 2

    def gather_rows(m, half, part):
        for index in range(2):
            if part < 2:
                bases = [((2 * pair + index) * 2 + half) * share * HALF for pair in range(2)]
                rows = jnp.concatenate(
                    [
                        turned_rows[pl.ds(base + part * few * HALF + m, few, stride=HALF), :]
                        for base in bases
                    ],
                    axis=0,
                )
            else:
                base = ((2 * part + index) * 2 + half) * share * HALF
                rows = turned_rows[pl.ds(base + m, share, stride=HALF), :]
            outgoing[part][2 * m + half, :, index * R : (index + 1) * R] = rows.astype(jnp.bfloat16)

    def send_half(step, half, part):
        to_tm, to_pair = owner_of(step)
        pltpu.make_async_remote_copy(
            src_ref=outgoing[part].at[(to_tm * 8 + to_pair) * 2 + half],
            dst_ref=received[part].at[here],
            send_sem=send_spectra.at[part],
            recv_sem=recv_spectra.at[part],
            device_id={"tm": to_tm, "chan": to_pair * 2 + half},
            device_id_type=MESH,
        ).start()

    def send_part(part):
        def one_chip(step, carry):
            to_tm, to_pair = owner_of(step)
            for half in range(2):
                gather_rows(to_tm * 8 + to_pair, half, part)
            for half in range(2):
                send_half(step, half, part)
            return carry

        lax.fori_loop(1, groups // 2, one_chip, 0)
        for half in range(2):
            gather_rows(tm * 8 + chan // 2, half, part)
        send_half(0, 1 - core, part)
        pltpu.make_async_copy(
            outgoing[part].at[tm * N_CHAN + chan], received[part].at[here], recv_spectra.at[part]
        ).start()

    lax.fori_loop(0, pieces // 2, one_piece, 0)
    pl.semaphore_wait(everyone_in, N_TIME - 1)
    send_part(0)
    lax.fori_loop(pieces // 2, pieces, one_piece, 0)
    for part in range(1, N_PARTS):
        send_part(part)

    def arrive(part):
        pltpu.make_async_copy(received[part], received[part], recv_spectra.at[part]).wait()

    block = sums_out.shape[2]
    columns = early_sums.shape[1] // block

    def first_column(j, carry):
        total = early_total.at[j]

        def emit(rows, sums, lower):
            total[rows, :] = sums if lower is None else jnp.where(lower, total[rows, :], sums)

        column_block(joined, rights[0], j, emit)
        return carry

    def sums_copy(j):
        some = pl.ds(pl.multiple_of(j * block, block), block)
        return pltpu.make_async_copy(sums_out.at[j % 2], early_sums.at[:, some], sums_sem.at[j % 2])

    def second_column(j, carry):
        @pl.when(j >= 2)
        def _():
            sums_copy(j - 2).wait()

        def emit(rows, sums, lower):
            slot = sums_out.at[j % 2]
            total = ((early_total[j, rows, :] + sums) * scale).astype(jnp.bfloat16)
            slot[rows, :] = total if lower is None else jnp.where(lower, slot[rows, :], total)

        column_block(earlies[2], rights[1], j, emit)
        sums_copy(j).start()
        return carry

    def join(slot, carry):
        rows = pl.ds(pl.multiple_of(slot * share, share), share)
        first_few, last_few = (earlies[part][rows, :].astype(jnp.float32) for part in range(2))
        for pair in range(2):
            some = slice(pair * few, (pair + 1) * few)
            both = jnp.concatenate([first_few[some], last_few[some]], axis=0)
            joined[rows, 2 * pair * R : 2 * (pair + 1) * R] = both.astype(jnp.bfloat16)
        return carry

    arrive(0)
    arrive(1)
    lax.fori_loop(0, groups, join, 0)
    lax.fori_loop(0, columns, first_column, 0)
    arrive(2)
    lax.fori_loop(0, columns, second_column, 0)
    sums_copy(columns - 2).wait()
    sums_copy(columns - 1).wait()

    sent = blocks.at[pl.ds(0, N_TIME - 1)]
    pltpu.make_async_copy(sent, sent, send_times).wait()
    for part in range(N_PARTS):
        sent = outgoing[part].at[pl.ds(0, groups - 1)]
        pltpu.make_async_copy(sent, sent, send_spectra.at[part]).wait()
    arrive(N_PARTS - 1)


def column_block(left, right, j, emit):
    signals, depth = left.shape
    block = right.shape[1]
    tall = signals
    here = pl.ds(pl.multiple_of(j * block, block), block)
    right[...] = left[here, :].T

    def product(rows):
        return jnp.dot(left[rows, :], right[...], preferred_element_type=jnp.float32)

    for m in range(signals // tall):
        rows = pl.ds(m * tall, tall)
        emit(rows, product(rows), None)
    own = left[here, :]
    for pair in range(depth // (2 * R)):
        real = slice(2 * pair * R, (2 * pair + 1) * R)
        imag = slice((2 * pair + 1) * R, (2 * pair + 2) * R)
        left[here, real] = own[:, imag]
        left[here, imag] = -own[:, real]
    shape = (block, block)
    lower = lax.broadcasted_iota(jnp.int32, shape, 0) >= lax.broadcasted_iota(jnp.int32, shape, 1)
    emit(here, product(here), lower)


def correlate_kernel(scale, late, early_sums, out, left, right, sums_in, result, late_sem, in_sem, out_sem):
    block = right.shape[1]
    columns = out.shape[2] // block

    def columns_of(j):
        return pl.ds(pl.multiple_of(j * block, block), block)

    def load(j):
        return pltpu.make_async_copy(early_sums.at[:, columns_of(j)], sums_in.at[j], in_sem.at[j])

    def store(j):
        return pltpu.make_async_copy(result.at[j], out.at[0, :, columns_of(j)], out_sem.at[j])

    load_left = pltpu.make_async_copy(late, left, late_sem)
    load_left.start()
    for j in range(columns):
        load(j).start()
    load_left.wait()

    def column(j, carry):
        load(j).wait()
        earlier, total = sums_in.at[j], result.at[j]

        def emit(rows, sums, lower):
            values = (sums * scale + earlier[rows, :].astype(jnp.float32)).astype(out.dtype)
            total[rows, :] = values if lower is None else jnp.where(lower, total[rows, :], values)

        column_block(left, right, j, emit)
        store(j).start()
        return carry

    lax.fori_loop(0, columns, column, 0)
    for j in range(columns):
        store(j).wait()


def shards(voltages, filter_taps, delays, dead_inputs):
    signals_here = voltages.shape[0]
    share = signals_here // N_TIME
    signals = signals_here * N_CHAN
    groups = N_TIME * N_CHAN
    in_hbm = pl.BlockSpec(memory_space=pltpu.HBM)
    pieces = 16
    block, last_block = 512, 512
    scale = 1.0 / (HALF * N_TIME)
    tables = dft_tables()

    late, early_sums = pl.pallas_call(
        functools.partial(channel_kernel, scale),
        out_shape=[
            jax.ShapeDtypeStruct((signals, 2 * R), jnp.bfloat16),
            jax.ShapeDtypeStruct((signals, signals), jnp.bfloat16),
        ],
        in_specs=[in_hbm] * 7,
        out_specs=[in_hbm, in_hbm],
        scratch_shapes=[
            pltpu.SMEM(delays.shape, jnp.int32),
            pltpu.SMEM(dead_inputs.shape, jnp.int32),
            pltpu.VMEM(filter_taps.shape, jnp.float32),
            *(pltpu.VMEM(table.shape, table.dtype) for table in tables),
            pltpu.VMEM(voltages.shape, jnp.bfloat16),
            pltpu.VMEM((R * share, R), jnp.float32),
            pltpu.VMEM((N_TIME, share, R, R), jnp.bfloat16),
            pltpu.VMEM((N_TIME, share, R, R), jnp.bfloat16),
            pltpu.VMEM((filter_taps.shape[0] * R, R), jnp.float32),
            pltpu.VMEM((2, share, HALF, R), jnp.float32),
            pltpu.VMEM((N_TIME * 2 * share * HALF, R), jnp.float32),
            [pltpu.VMEM((groups, share, 2 * R), jnp.bfloat16)] * N_PARTS,
            [pltpu.VMEM((signals, 2 * R), jnp.bfloat16)] * (N_PARTS - 1),
            pltpu.VMEM((signals, 4 * R), jnp.bfloat16),
            [pltpu.VMEM((depth, block), jnp.bfloat16) for depth in (4 * R, 2 * R)],
            pltpu.VMEM((signals // block, signals, block), jnp.float32),
            pltpu.VMEM((2, signals, block), jnp.bfloat16),
            pltpu.SemaphoreType.DMA((3 + len(tables),)),
            pltpu.SemaphoreType.DMA((N_TIME,)),
            pltpu.SemaphoreType.DMA,
            pltpu.SemaphoreType.DMA((pieces,)),
            pltpu.SemaphoreType.DMA((N_PARTS,)),
            pltpu.SemaphoreType.DMA((N_PARTS,)),
            pltpu.SemaphoreType.DMA((2,)),
            pltpu.SemaphoreType.REGULAR,
        ],
        compiler_params=pltpu.CompilerParams(collective_id=0, has_side_effects=True, vmem_limit_bytes=VMEM_LIMIT),
        name="channels",
    )(voltages, delays, dead_inputs, filter_taps, *tables)

    return pl.pallas_call(
        functools.partial(correlate_kernel, scale),
        out_shape=jax.ShapeDtypeStruct((1, signals, signals), jnp.bfloat16),
        in_specs=[in_hbm, in_hbm],
        out_specs=in_hbm,
        scratch_shapes=[
            pltpu.VMEM((signals, 2 * R), jnp.bfloat16),
            pltpu.VMEM((2 * R, last_block), jnp.bfloat16),
            pltpu.VMEM((signals // last_block, signals, last_block), jnp.bfloat16),
            pltpu.VMEM((signals // last_block, signals, last_block), jnp.bfloat16),
            pltpu.SemaphoreType.DMA,
            pltpu.SemaphoreType.DMA((signals // last_block,)),
            pltpu.SemaphoreType.DMA((signals // last_block,)),
        ],
        compiler_params=pltpu.CompilerParams(vmem_limit_bytes=VMEM_LIMIT),
        name="correlate",
    )(late, early_sums)


def solution(mesh):
    in_specs = (P("chan", "tm"), P(), P("chan"), P("chan"))
    out_specs = P(("tm", "chan"), None, None)
    return jax.shard_map(shards, mesh=mesh, in_specs=in_specs, out_specs=out_specs, check_vma=False)
```

```python
import functools

import jax
import jax.numpy as jnp
import numpy as np
from jax import lax
from jax.experimental import pallas as pl
from jax.experimental.pallas import tpu as pltpu
from jax.sharding import PartitionSpec as P

R = 128
HALF = R // 2
N_TIME = 8
N_CHAN = 16
VMEM_LIMIT = 60 * 2**20
N_PARTS = 4
MESH = pl.DeviceIdType.MESH
two_pi = 2.0 * np.pi


def dft_tables():
    indices = np.arange(R)
    outer = indices[:, None] * indices[None, :]
    angles = two_pi / R * (outer % R)
    cos, sin = np.cos(angles), np.sin(angles)
    first = np.concatenate([cos, -sin], axis=0)
    twist = two_pi / (R * R) * outer
    cos_m, sin_m = cos[:HALF], sin[:HALF]
    second = np.concatenate(
        [np.concatenate([cos_m, sin_m], axis=1), np.concatenate([-sin_m, cos_m], axis=1)], axis=0
    )
    return (
        jnp.asarray(first, jnp.bfloat16),
        jnp.asarray(np.stack([np.cos(twist), np.sin(twist)]), jnp.float32),
        jnp.asarray(second, jnp.bfloat16),
    )


def place():
    tm, chan = lax.axis_index("tm"), lax.axis_index("chan")
    return 2 * (tm // 4) + chan // 2 % 2, tm % 4, chan // 4, chan % 2


def channel_kernel(
    scale,
    volts, delays_in, dead_in, taps_in, first_in, twist_in, second_in,
    late, early_sums,
    delays, dead_inputs, raw_taps, first, twist, second,
    own, wide, blocks, times, taps, rot, turned_rows, outgoing,
    earlies, joined, rights, early_total, sums_out,
    table_sem, load_sem, send_times, recv_times, send_spectra, recv_spectra, sums_sem, everyone_in,
):
    share = times.shape[1]
    n_taps = raw_taps.shape[0]
    pieces = recv_times.shape[0]
    per = share // pieces
    groups = outgoing[0].shape[0]
    tm, chan = lax.axis_index("tm"), lax.axis_index("chan")

    barrier = pltpu.get_barrier_semaphore()

    def greet(sem, axis, size):
        def one(step, carry):
            other = lax.rem(lax.axis_index(axis) + step, size)
            pl.semaphore_signal(sem, inc=1, device_id={axis: other}, device_id_type=MESH)
            return carry

        lax.fori_loop(1, size, one, 0)

    def partner(step):
        along_y = step % 4
        across = step // 4
        return (tm // 4 + across) % 2 * 4 + (tm + along_y) % 4

    def rows_of(owner):
        return pl.ds(pl.multiple_of(owner * share, share), share)

    def load(step):
        rows = rows_of(partner(step % N_TIME))
        return pltpu.make_async_copy(volts.at[rows], own.at[rows], load_sem.at[step % N_TIME])

    def start_load(step, carry):
        load(step).start()
        return carry

    def spread(owner, target):
        rows = rows_of(owner)
        for a in range(R):
            wide[a * share : (a + 1) * share, :] = own[rows, a * R : (a + 1) * R].astype(jnp.float32)
        for s in range(share):
            target[s] = wide[pl.ds(s, R, stride=share), :].astype(jnp.bfloat16)

    def send_piece(step, piece):
        owner = partner(step)
        some = pl.ds(piece * per, per)
        pltpu.make_async_remote_copy(
            src_ref=blocks.at[owner, some],
            dst_ref=times.at[tm, some],
            send_sem=send_times,
            recv_sem=recv_times.at[piece],
            device_id={"tm": owner},
            device_id_type=MESH,
        ).start()

    def first_piece(step, carry):
        owner = partner(step)
        load(step).wait()
        spread(owner, blocks.at[owner])

        @pl.when(step == 1)
        def _():
            pl.semaphore_wait(barrier, N_TIME - 1 + N_CHAN - 1)

        send_piece(step, 0)
        return carry

    lax.fori_loop(1, N_TIME + 1, start_load, 0)
    greet(barrier, "tm", N_TIME)
    greet(barrier, "chan", N_CHAN)
    sources = (delays_in, dead_in, taps_in, first_in, twist_in, second_in)
    places = (delays, dead_inputs, raw_taps, first, twist, second)
    tables = [
        pltpu.make_async_copy(source, place, table_sem.at[index])
        for index, (source, place) in enumerate(zip(sources, places))
    ]
    for table in tables:
        table.start()
    lax.fori_loop(1, N_TIME, first_piece, 0)

    def later_piece(index, carry):
        send_piece(index % (N_TIME - 1) + 1, index // (N_TIME - 1) + 1)
        return carry

    lax.fori_loop(0, (N_TIME - 1) * (pieces - 1), later_piece, 0)

    greet(everyone_in, "tm", N_TIME)
    load(0).wait()
    spread(tm, times.at[tm])

    for table in tables:
        table.wait()
    for a in range(R):
        taps[pl.ds(a, n_taps, stride=R), :] = raw_taps[:, a * R : (a + 1) * R]
    channels = lax.broadcasted_iota(jnp.int32, (HALF, R), 0) * R + lax.broadcasted_iota(
        jnp.int32, (HALF, R), 1
    )

    def one_rotation(s, carry):
        phases = (two_pi / (R * R)) * (channels * delays[tm * share + s] & (R * R - 1)).astype(jnp.float32)
        weight = (1 - dead_inputs[tm * share + s]).astype(jnp.float32) / R
        rot[0, s] = jnp.cos(phases) * weight
        rot[1, s] = jnp.sin(phases) * weight
        return carry

    lax.fori_loop(0, share, one_rotation, 0)

    low = lax.broadcasted_iota(jnp.int32, (HALF, R), 1) < HALF

    def one_signal(s, carry):
        spectrum = [None] * N_TIME
        for t in range(N_TIME):
            filtered = taps[:R] * times[t, s].astype(jnp.float32)
            for j in range(1, min(n_taps, t + 1)):
                filtered = filtered + taps[j * R : (j + 1) * R] * times[t - j, s].astype(jnp.float32)
            sums = jnp.dot(
                first[...], filtered.astype(jnp.bfloat16), preferred_element_type=jnp.float32
            )
            real, imag = sums[:R], sums[R:]
            turned = jnp.concatenate(
                [
                    (real * twist[0] + imag * twist[1]).astype(jnp.bfloat16),
                    (imag * twist[0] - real * twist[1]).astype(jnp.bfloat16),
                ],
                axis=1,
            )
            raw = lax.dot_general(
                second[...],
                turned,
                (((1,), (1,)), ((), ())),
                preferred_element_type=jnp.float32,
            )
            rot_cos, rot_sin = rot[0, s], rot[1, s]
            spectrum[t] = (
                raw[:HALF] * rot_cos - raw[HALF:] * rot_sin,
                raw[:HALF] * rot_sin + raw[HALF:] * rot_cos,
            )
            if t % 2 == 1:
                for part in range(2):
                    even, odd = spectrum[t - 1][part], spectrum[t][part]
                    lower = jnp.where(low, even, pltpu.roll(odd, HALF, 1))
                    upper = jnp.where(low, pltpu.roll(even, HALF, 1), odd)
                    tile = (t // 2) * 2 + part
                    for half, value in enumerate((lower, upper)):
                        row = ((tile * 2 + half) * share + s) * HALF
                        turned_rows[pl.ds(pl.multiple_of(row, HALF), HALF), :] = value
        return carry

    def one_piece(piece, carry):
        arrived = times.at[pl.ds(0, N_TIME - 1), pl.ds(piece * per, per)]
        pltpu.make_async_copy(arrived, arrived, recv_times.at[piece]).wait()
        lax.fori_loop(piece * per, (piece + 1) * per, one_signal, 0)
        return carry

    here = pl.ds(pl.multiple_of((chan * N_TIME + tm) * share, share), share)
    x, y, z, core = place()

    def owner_of(step):
        to_x = (x + step // 16 + step) % 4
        to_y = (y + step) % 4
        to_z = (z + step // 4 + step) % 4
        return to_x // 2 * 4 + to_y, to_z * 2 + to_x % 2

    received = (*earlies, late)
    few = share // 2

    def gather_rows(m, half, part):
        for index in range(2):
            if part < 2:
                bases = [((2 * pair + index) * 2 + half) * share * HALF for pair in range(2)]
                rows = jnp.concatenate(
                    [
                        turned_rows[pl.ds(base + part * few * HALF + m, few, stride=HALF), :]
                        for base in bases
                    ],
                    axis=0,
                )
            else:
                base = ((2 * part + index) * 2 + half) * share * HALF
                rows = turned_rows[pl.ds(base + m, share, stride=HALF), :]
            outgoing[part][2 * m + half, :, index * R : (index + 1) * R] = rows.astype(jnp.bfloat16)

    def send_half(step, half, part):
        to_tm, to_pair = owner_of(step)
        pltpu.make_async_remote_copy(
            src_ref=outgoing[part].at[(to_tm * 8 + to_pair) * 2 + half],
            dst_ref=received[part].at[here],
            send_sem=send_spectra.at[part],
            recv_sem=recv_spectra.at[part],
            device_id={"tm": to_tm, "chan": to_pair * 2 + half},
            device_id_type=MESH,
        ).start()

    def send_part(part):
        def one_chip(step, carry):
            to_tm, to_pair = owner_of(step)
            for half in range(2):
                gather_rows(to_tm * 8 + to_pair, half, part)
            for half in range(2):
                send_half(step, half, part)
            return carry

        lax.fori_loop(1, groups // 2, one_chip, 0)
        for half in range(2):
            gather_rows(tm * 8 + chan // 2, half, part)
        send_half(0, 1 - core, part)
        pltpu.make_async_copy(
            outgoing[part].at[tm * N_CHAN + chan], received[part].at[here], recv_spectra.at[part]
        ).start()

    lax.fori_loop(0, pieces // 2, one_piece, 0)
    pl.semaphore_wait(everyone_in, N_TIME - 1)
    send_part(0)
    lax.fori_loop(pieces // 2, pieces, one_piece, 0)
    for part in range(1, N_PARTS):
        send_part(part)

    def arrive(part):
        pltpu.make_async_copy(received[part], received[part], recv_spectra.at[part]).wait()

    block = sums_out.shape[2]
    columns = early_sums.shape[1] // block

    def first_column(j, carry):
        total = early_total.at[j]

        def emit(rows, sums, lower):
            total[rows, :] = sums if lower is None else jnp.where(lower, total[rows, :], sums)

        column_block(joined, rights[0], j, emit)
        return carry

    def sums_copy(j):
        some = pl.ds(pl.multiple_of(j * block, block), block)
        return pltpu.make_async_copy(sums_out.at[j % 2], early_sums.at[:, some], sums_sem.at[j % 2])

    def second_column(j, carry):
        @pl.when(j >= 2)
        def _():
            sums_copy(j - 2).wait()

        def emit(rows, sums, lower):
            slot = sums_out.at[j % 2]
            total = ((early_total[j, rows, :] + sums) * scale).astype(jnp.bfloat16)
            slot[rows, :] = total if lower is None else jnp.where(lower, slot[rows, :], total)

        column_block(earlies[2], rights[1], j, emit)
        sums_copy(j).start()
        return carry

    def join(slot, carry):
        rows = pl.ds(pl.multiple_of(slot * share, share), share)
        first_few, last_few = (earlies[part][rows, :].astype(jnp.float32) for part in range(2))
        for pair in range(2):
            some = slice(pair * few, (pair + 1) * few)
            both = jnp.concatenate([first_few[some], last_few[some]], axis=0)
            joined[rows, 2 * pair * R : 2 * (pair + 1) * R] = both.astype(jnp.bfloat16)
        return carry

    arrive(0)
    arrive(1)
    lax.fori_loop(0, groups, join, 0)
    lax.fori_loop(0, columns, first_column, 0)
    arrive(2)
    lax.fori_loop(0, columns, second_column, 0)
    sums_copy(columns - 2).wait()
    sums_copy(columns - 1).wait()

    sent = blocks.at[pl.ds(0, N_TIME - 1)]
    pltpu.make_async_copy(sent, sent, send_times).wait()
    for part in range(N_PARTS):
        sent = outgoing[part].at[pl.ds(0, groups - 1)]
        pltpu.make_async_copy(sent, sent, send_spectra.at[part]).wait()
    arrive(N_PARTS - 1)


def column_block(left, right, j, emit):
    signals, depth = left.shape
    block = right.shape[1]
    tall = signals
    here = pl.ds(pl.multiple_of(j * block, block), block)
    right[...] = left[here, :].T

    def product(rows):
        return jnp.dot(left[rows, :], right[...], preferred_element_type=jnp.float32)

    for m in range(signals // tall):
        rows = pl.ds(m * tall, tall)
        emit(rows, product(rows), None)
    own = left[here, :]
    for pair in range(depth // (2 * R)):
        real = slice(2 * pair * R, (2 * pair + 1) * R)
        imag = slice((2 * pair + 1) * R, (2 * pair + 2) * R)
        left[here, real] = own[:, imag]
        left[here, imag] = -own[:, real]
    shape = (block, block)
    lower = lax.broadcasted_iota(jnp.int32, shape, 0) >= lax.broadcasted_iota(jnp.int32, shape, 1)
    emit(here, product(here), lower)


def correlate_kernel(scale, late, early_sums, out, left, right, sums_in, result, late_sem, in_sem, out_sem):
    block = right.shape[1]
    columns = out.shape[2] // block

    def columns_of(j):
        return pl.ds(pl.multiple_of(j * block, block), block)

    def load(j):
        return pltpu.make_async_copy(early_sums.at[:, columns_of(j)], sums_in.at[j], in_sem.at[j])

    def store(j):
        return pltpu.make_async_copy(result.at[j], out.at[0, :, columns_of(j)], out_sem.at[j])

    load_left = pltpu.make_async_copy(late, left, late_sem)
    load_left.start()
    for j in range(columns):
        load(j).start()
    load_left.wait()

    def column(j, carry):
        load(j).wait()
        earlier, total = sums_in.at[j], result.at[j]

        def emit(rows, sums, lower):
            values = (sums * scale + earlier[rows, :].astype(jnp.float32)).astype(out.dtype)
            total[rows, :] = values if lower is None else jnp.where(lower, total[rows, :], values)

        column_block(left, right, j, emit)
        store(j).start()
        return carry

    lax.fori_loop(0, columns, column, 0)
    for j in range(columns):
        store(j).wait()


def shards(voltages, filter_taps, delays, dead_inputs):
    signals_here = voltages.shape[0]
    share = signals_here // N_TIME
    signals = signals_here * N_CHAN
    groups = N_TIME * N_CHAN
    in_hbm = pl.BlockSpec(memory_space=pltpu.HBM)
    pieces = 8
    block, last_block = 512, 512
    scale = 1.0 / (HALF * N_TIME)
    tables = dft_tables()

    late, early_sums = pl.pallas_call(
        functools.partial(channel_kernel, scale),
        out_shape=[
            jax.ShapeDtypeStruct((signals, 2 * R), jnp.bfloat16),
            jax.ShapeDtypeStruct((signals, signals), jnp.bfloat16),
        ],
        in_specs=[in_hbm] * 7,
        out_specs=[in_hbm, in_hbm],
        scratch_shapes=[
            pltpu.SMEM(delays.shape, jnp.int32),
            pltpu.SMEM(dead_inputs.shape, jnp.int32),
            pltpu.VMEM(filter_taps.shape, jnp.float32),
            *(pltpu.VMEM(table.shape, table.dtype) for table in tables),
            pltpu.VMEM(voltages.shape, jnp.bfloat16),
            pltpu.VMEM((R * share, R), jnp.float32),
            pltpu.VMEM((N_TIME, share, R, R), jnp.bfloat16),
            pltpu.VMEM((N_TIME, share, R, R), jnp.bfloat16),
            pltpu.VMEM((filter_taps.shape[0] * R, R), jnp.float32),
            pltpu.VMEM((2, share, HALF, R), jnp.float32),
            pltpu.VMEM((N_TIME * 2 * share * HALF, R), jnp.float32),
            [pltpu.VMEM((groups, share, 2 * R), jnp.bfloat16)] * N_PARTS,
            [pltpu.VMEM((signals, 2 * R), jnp.bfloat16)] * (N_PARTS - 1),
            pltpu.VMEM((signals, 4 * R), jnp.bfloat16),
            [pltpu.VMEM((depth, block), jnp.bfloat16) for depth in (4 * R, 2 * R)],
            pltpu.VMEM((signals // block, signals, block), jnp.float32),
            pltpu.VMEM((2, signals, block), jnp.bfloat16),
            pltpu.SemaphoreType.DMA((3 + len(tables),)),
            pltpu.SemaphoreType.DMA((N_TIME,)),
            pltpu.SemaphoreType.DMA,
            pltpu.SemaphoreType.DMA((pieces,)),
            pltpu.SemaphoreType.DMA((N_PARTS,)),
            pltpu.SemaphoreType.DMA((N_PARTS,)),
            pltpu.SemaphoreType.DMA((2,)),
            pltpu.SemaphoreType.REGULAR,
        ],
        compiler_params=pltpu.CompilerParams(collective_id=0, has_side_effects=True, vmem_limit_bytes=VMEM_LIMIT),
        name="channels",
    )(voltages, delays, dead_inputs, filter_taps, *tables)

    return pl.pallas_call(
        functools.partial(correlate_kernel, scale),
        out_shape=jax.ShapeDtypeStruct((1, signals, signals), jnp.bfloat16),
        in_specs=[in_hbm, in_hbm],
        out_specs=in_hbm,
        scratch_shapes=[
            pltpu.VMEM((signals, 2 * R), jnp.bfloat16),
            pltpu.VMEM((2 * R, last_block), jnp.bfloat16),
            pltpu.VMEM((signals // last_block, signals, last_block), jnp.bfloat16),
            pltpu.VMEM((signals // last_block, signals, last_block), jnp.bfloat16),
            pltpu.SemaphoreType.DMA,
            pltpu.SemaphoreType.DMA((signals // last_block,)),
            pltpu.SemaphoreType.DMA((signals // last_block,)),
        ],
        compiler_params=pltpu.CompilerParams(vmem_limit_bytes=VMEM_LIMIT),
        name="correlate",
    )(late, early_sums)


def solution(mesh):
    in_specs = (P("chan", "tm"), P(), P("chan"), P("chan"))
    out_specs = P(("tm", "chan"), None, None)
    return jax.shard_map(shards, mesh=mesh, in_specs=in_specs, out_specs=out_specs, check_vma=False)
```

```python
import functools

import jax
import jax.numpy as jnp
import numpy as np
from jax import lax
from jax.experimental import pallas as pl
from jax.experimental.pallas import tpu as pltpu
from jax.sharding import PartitionSpec as P

R = 128
HALF = R // 2
N_TIME = 8
N_CHAN = 16
VMEM_LIMIT = 60 * 2**20
N_PARTS = 4
MESH = pl.DeviceIdType.MESH
two_pi = 2.0 * np.pi


def dft_tables():
    indices = np.arange(R)
    outer = indices[:, None] * indices[None, :]
    angles = two_pi / R * (outer % R)
    cos, sin = np.cos(angles), np.sin(angles)
    first = np.concatenate([cos, -sin], axis=0)
    twist = two_pi / (R * R) * outer
    cos_m, sin_m = cos[:HALF], sin[:HALF]
    second = np.concatenate(
        [np.concatenate([cos_m, sin_m], axis=1), np.concatenate([-sin_m, cos_m], axis=1)], axis=0
    )
    return (
        jnp.asarray(first, jnp.bfloat16),
        jnp.asarray(np.stack([np.cos(twist), np.sin(twist)]), jnp.float32),
        jnp.asarray(second, jnp.bfloat16),
    )


def place():
    tm, chan = lax.axis_index("tm"), lax.axis_index("chan")
    return 2 * (tm // 4) + chan // 2 % 2, tm % 4, chan // 4, chan % 2


def channel_kernel(
    scale,
    volts, delays_in, dead_in, taps_in, first_in, twist_in, second_in,
    late, early_sums,
    delays, dead_inputs, raw_taps, first, twist, second,
    own, wide, blocks, times, taps, rot, turned_rows, outgoing,
    earlies, joined, rights, early_total, sums_out,
    table_sem, load_sem, send_times, recv_times, send_spectra, recv_spectra, sums_sem, everyone_in,
):
    share = times.shape[1]
    n_taps = raw_taps.shape[0]
    pieces = recv_times.shape[0]
    per = share // pieces
    groups = outgoing[0].shape[0]
    tm, chan = lax.axis_index("tm"), lax.axis_index("chan")

    barrier = pltpu.get_barrier_semaphore()

    def greet(sem, axis, size):
        def one(step, carry):
            other = lax.rem(lax.axis_index(axis) + step, size)
            pl.semaphore_signal(sem, inc=1, device_id={axis: other}, device_id_type=MESH)
            return carry

        lax.fori_loop(1, size, one, 0)

    def partner(step):
        along_y = step % 4
        across = step // 4
        return (tm // 4 + across) % 2 * 4 + (tm + along_y) % 4

    def rows_of(owner):
        return pl.ds(pl.multiple_of(owner * share, share), share)

    def load(step):
        rows = rows_of(partner(step % N_TIME))
        return pltpu.make_async_copy(volts.at[rows], own.at[rows], load_sem.at[step % N_TIME])

    def start_load(step, carry):
        load(step).start()
        return carry

    def spread(owner, target):
        rows = rows_of(owner)
        for a in range(R):
            wide[a * share : (a + 1) * share, :] = own[rows, a * R : (a + 1) * R].astype(jnp.float32)
        for s in range(share):
            target[s] = wide[pl.ds(s, R, stride=share), :].astype(jnp.bfloat16)

    def send_piece(step, piece):
        owner = partner(step)
        some = pl.ds(piece * per, per)
        pltpu.make_async_remote_copy(
            src_ref=blocks.at[owner, some],
            dst_ref=times.at[tm, some],
            send_sem=send_times,
            recv_sem=recv_times.at[piece],
            device_id={"tm": owner},
            device_id_type=MESH,
        ).start()

    def first_piece(step, carry):
        owner = partner(step)
        load(step).wait()
        spread(owner, blocks.at[owner])

        @pl.when(step == 1)
        def _():
            pl.semaphore_wait(barrier, N_TIME - 1 + N_CHAN - 1)

        send_piece(step, 0)
        return carry

    lax.fori_loop(1, N_TIME + 1, start_load, 0)
    greet(barrier, "tm", N_TIME)
    greet(barrier, "chan", N_CHAN)
    sources = (delays_in, dead_in, taps_in, first_in, twist_in, second_in)
    places = (delays, dead_inputs, raw_taps, first, twist, second)
    tables = [
        pltpu.make_async_copy(source, place, table_sem.at[index])
        for index, (source, place) in enumerate(zip(sources, places))
    ]
    for table in tables:
        table.start()
    lax.fori_loop(1, N_TIME, first_piece, 0)

    def later_piece(index, carry):
        send_piece(index % (N_TIME - 1) + 1, index // (N_TIME - 1) + 1)
        return carry

    lax.fori_loop(0, (N_TIME - 1) * (pieces - 1), later_piece, 0)

    greet(everyone_in, "tm", N_TIME)
    load(0).wait()
    spread(tm, times.at[tm])

    for table in tables:
        table.wait()
    for a in range(R):
        taps[pl.ds(a, n_taps, stride=R), :] = raw_taps[:, a * R : (a + 1) * R]
    channels = lax.broadcasted_iota(jnp.int32, (HALF, R), 0) * R + lax.broadcasted_iota(
        jnp.int32, (HALF, R), 1
    )

    def one_rotation(s, carry):
        phases = (two_pi / (R * R)) * (channels * delays[tm * share + s] & (R * R - 1)).astype(jnp.float32)
        weight = (1 - dead_inputs[tm * share + s]).astype(jnp.float32) / R
        rot[0, s] = jnp.cos(phases) * weight
        rot[1, s] = jnp.sin(phases) * weight
        return carry

    lax.fori_loop(0, share, one_rotation, 0)

    low = lax.broadcasted_iota(jnp.int32, (HALF, R), 1) < HALF

    def one_signal(s, carry):
        spectrum = [None] * N_TIME
        for t in range(N_TIME):
            filtered = taps[:R] * times[t, s].astype(jnp.float32)
            for j in range(1, min(n_taps, t + 1)):
                filtered = filtered + taps[j * R : (j + 1) * R] * times[t - j, s].astype(jnp.float32)
            sums = jnp.dot(
                first[...], filtered.astype(jnp.bfloat16), preferred_element_type=jnp.float32
            )
            real, imag = sums[:R], sums[R:]
            turned = jnp.concatenate(
                [
                    (real * twist[0] + imag * twist[1]).astype(jnp.bfloat16),
                    (imag * twist[0] - real * twist[1]).astype(jnp.bfloat16),
                ],
                axis=1,
            )
            raw = lax.dot_general(
                second[...],
                turned,
                (((1,), (1,)), ((), ())),
                preferred_element_type=jnp.float32,
            )
            rot_cos, rot_sin = rot[0, s], rot[1, s]
            spectrum[t] = (
                raw[:HALF] * rot_cos - raw[HALF:] * rot_sin,
                raw[:HALF] * rot_sin + raw[HALF:] * rot_cos,
            )
            if t % 2 == 1:
                for part in range(2):
                    even, odd = spectrum[t - 1][part], spectrum[t][part]
                    lower = jnp.where(low, even, pltpu.roll(odd, HALF, 1))
                    upper = jnp.where(low, pltpu.roll(even, HALF, 1), odd)
                    tile = (t // 2) * 2 + part
                    for half, value in enumerate((lower, upper)):
                        row = ((tile * 2 + half) * share + s) * HALF
                        turned_rows[pl.ds(pl.multiple_of(row, HALF), HALF), :] = value
        return carry

    def one_piece(piece, carry):
        arrived = times.at[pl.ds(0, N_TIME - 1), pl.ds(piece * per, per)]
        pltpu.make_async_copy(arrived, arrived, recv_times.at[piece]).wait()
        lax.fori_loop(piece * per, (piece + 1) * per, one_signal, 0)
        return carry

    here = pl.ds(pl.multiple_of((chan * N_TIME + tm) * share, share), share)
    x, y, z, core = place()

    def owner_of(step):
        to_x = (x + step // 16 + step) % 4
        to_y = (y + step) % 4
        to_z = (z + step // 4 + step) % 4
        return to_x // 2 * 4 + to_y, to_z * 2 + to_x % 2

    received = (*earlies, late)
    few = share // 2

    def gather_rows(m, half, part):
        for index in range(2):
            if part < 2:
                bases = [((2 * pair + index) * 2 + half) * share * HALF for pair in range(2)]
                rows = jnp.concatenate(
                    [
                        turned_rows[pl.ds(base + part * few * HALF + m, few, stride=HALF), :]
                        for base in bases
                    ],
                    axis=0,
                )
            else:
                base = ((2 * part + index) * 2 + half) * share * HALF
                rows = turned_rows[pl.ds(base + m, share, stride=HALF), :]
            outgoing[part][2 * m + half, :, index * R : (index + 1) * R] = rows.astype(jnp.bfloat16)

    def send_half(step, half, part):
        to_tm, to_pair = owner_of(step)
        pltpu.make_async_remote_copy(
            src_ref=outgoing[part].at[(to_tm * 8 + to_pair) * 2 + half],
            dst_ref=received[part].at[here],
            send_sem=send_spectra.at[part],
            recv_sem=recv_spectra.at[part],
            device_id={"tm": to_tm, "chan": to_pair * 2 + half},
            device_id_type=MESH,
        ).start()

    def send_part(part):
        def one_chip(step, carry):
            to_tm, to_pair = owner_of(step)
            for half in range(2):
                gather_rows(to_tm * 8 + to_pair, half, part)
            for half in range(2):
                send_half(step, half, part)
            return carry

        lax.fori_loop(1, groups // 2, one_chip, 0)
        for half in range(2):
            gather_rows(tm * 8 + chan // 2, half, part)
        send_half(0, 1 - core, part)
        pltpu.make_async_copy(
            outgoing[part].at[tm * N_CHAN + chan], received[part].at[here], recv_spectra.at[part]
        ).start()

    lax.fori_loop(0, pieces // 2, one_piece, 0)
    pl.semaphore_wait(everyone_in, N_TIME - 1)
    send_part(0)
    lax.fori_loop(pieces // 2, pieces, one_piece, 0)
    for part in range(1, N_PARTS):
        send_part(part)

    def arrive(part):
        pltpu.make_async_copy(received[part], received[part], recv_spectra.at[part]).wait()

    block = sums_out.shape[2]
    columns = early_sums.shape[1] // block

    def first_column(j, carry):
        total = early_total.at[j]

        def emit(rows, sums, lower):
            total[rows, :] = sums if lower is None else jnp.where(lower, total[rows, :], sums)

        column_block(joined, rights[0], j, emit)
        return carry

    def sums_copy(j):
        some = pl.ds(pl.multiple_of(j * block, block), block)
        return pltpu.make_async_copy(sums_out.at[j % 2], early_sums.at[:, some], sums_sem.at[j % 2])

    def second_column(j, carry):
        @pl.when(j >= 2)
        def _():
            sums_copy(j - 2).wait()

        def emit(rows, sums, lower):
            slot = sums_out.at[j % 2]
            total = ((early_total[j, rows, :] + sums) * scale).astype(jnp.bfloat16)
            slot[rows, :] = total if lower is None else jnp.where(lower, slot[rows, :], total)

        column_block(earlies[2], rights[1], j, emit)
        sums_copy(j).start()
        return carry

    def join(slot, carry):
        rows = pl.ds(pl.multiple_of(slot * share, share), share)
        first_few, last_few = (earlies[part][rows, :].astype(jnp.float32) for part in range(2))
        for pair in range(2):
            some = slice(pair * few, (pair + 1) * few)
            both = jnp.concatenate([first_few[some], last_few[some]], axis=0)
            joined[rows, 2 * pair * R : 2 * (pair + 1) * R] = both.astype(jnp.bfloat16)
        return carry

    arrive(0)
    arrive(1)
    lax.fori_loop(0, groups, join, 0)
    lax.fori_loop(0, columns, first_column, 0)
    arrive(2)
    lax.fori_loop(0, columns, second_column, 0)
    sums_copy(columns - 2).wait()
    sums_copy(columns - 1).wait()

    sent = blocks.at[pl.ds(0, N_TIME - 1)]
    pltpu.make_async_copy(sent, sent, send_times).wait()
    for part in range(N_PARTS):
        sent = outgoing[part].at[pl.ds(0, groups - 1)]
        pltpu.make_async_copy(sent, sent, send_spectra.at[part]).wait()
    arrive(N_PARTS - 1)


def column_block(left, right, j, emit):
    signals, depth = left.shape
    block = right.shape[0]
    tall = signals
    here = pl.ds(pl.multiple_of(j * block, block), block)
    right[...] = left[here, :]

    def product(rows):
        return lax.dot_general(
            left[rows, :], right[...], (((1,), (1,)), ((), ())), preferred_element_type=jnp.float32
        )

    for m in range(signals // tall):
        rows = pl.ds(m * tall, tall)
        emit(rows, product(rows), None)
    own = left[here, :]
    for pair in range(depth // (2 * R)):
        real = slice(2 * pair * R, (2 * pair + 1) * R)
        imag = slice((2 * pair + 1) * R, (2 * pair + 2) * R)
        left[here, real] = own[:, imag]
        left[here, imag] = -own[:, real]
    shape = (block, block)
    lower = lax.broadcasted_iota(jnp.int32, shape, 0) >= lax.broadcasted_iota(jnp.int32, shape, 1)
    emit(here, product(here), lower)


def correlate_kernel(scale, late, early_sums, out, left, right, sums_in, result, late_sem, in_sem, out_sem):
    block = right.shape[0]
    columns = out.shape[2] // block

    def columns_of(j):
        return pl.ds(pl.multiple_of(j * block, block), block)

    def load(j):
        return pltpu.make_async_copy(early_sums.at[:, columns_of(j)], sums_in.at[j], in_sem.at[j])

    def store(j):
        return pltpu.make_async_copy(result.at[j], out.at[0, :, columns_of(j)], out_sem.at[j])

    load_left = pltpu.make_async_copy(late, left, late_sem)
    load_left.start()
    for j in range(columns):
        load(j).start()
    load_left.wait()

    def column(j, carry):
        load(j).wait()
        earlier, total = sums_in.at[j], result.at[j]

        def emit(rows, sums, lower):
            values = (sums * scale + earlier[rows, :].astype(jnp.float32)).astype(out.dtype)
            total[rows, :] = values if lower is None else jnp.where(lower, total[rows, :], values)

        column_block(left, right, j, emit)
        store(j).start()
        return carry

    lax.fori_loop(0, columns, column, 0)
    for j in range(columns):
        store(j).wait()


def shards(voltages, filter_taps, delays, dead_inputs):
    signals_here = voltages.shape[0]
    share = signals_here // N_TIME
    signals = signals_here * N_CHAN
    groups = N_TIME * N_CHAN
    in_hbm = pl.BlockSpec(memory_space=pltpu.HBM)
    pieces = 8
    block, last_block = 512, 512
    scale = 1.0 / (HALF * N_TIME)
    tables = dft_tables()

    late, early_sums = pl.pallas_call(
        functools.partial(channel_kernel, scale),
        out_shape=[
            jax.ShapeDtypeStruct((signals, 2 * R), jnp.bfloat16),
            jax.ShapeDtypeStruct((signals, signals), jnp.bfloat16),
        ],
        in_specs=[in_hbm] * 7,
        out_specs=[in_hbm, in_hbm],
        scratch_shapes=[
            pltpu.SMEM(delays.shape, jnp.int32),
            pltpu.SMEM(dead_inputs.shape, jnp.int32),
            pltpu.VMEM(filter_taps.shape, jnp.float32),
            *(pltpu.VMEM(table.shape, table.dtype) for table in tables),
            pltpu.VMEM(voltages.shape, jnp.bfloat16),
            pltpu.VMEM((R * share, R), jnp.float32),
            pltpu.VMEM((N_TIME, share, R, R), jnp.bfloat16),
            pltpu.VMEM((N_TIME, share, R, R), jnp.bfloat16),
            pltpu.VMEM((filter_taps.shape[0] * R, R), jnp.float32),
            pltpu.VMEM((2, share, HALF, R), jnp.float32),
            pltpu.VMEM((N_TIME * 2 * share * HALF, R), jnp.float32),
            [pltpu.VMEM((groups, share, 2 * R), jnp.bfloat16)] * N_PARTS,
            [pltpu.VMEM((signals, 2 * R), jnp.bfloat16)] * (N_PARTS - 1),
            pltpu.VMEM((signals, 4 * R), jnp.bfloat16),
            [pltpu.VMEM((block, depth), jnp.bfloat16) for depth in (4 * R, 2 * R)],
            pltpu.VMEM((signals // block, signals, block), jnp.float32),
            pltpu.VMEM((2, signals, block), jnp.bfloat16),
            pltpu.SemaphoreType.DMA((3 + len(tables),)),
            pltpu.SemaphoreType.DMA((N_TIME,)),
            pltpu.SemaphoreType.DMA,
            pltpu.SemaphoreType.DMA((pieces,)),
            pltpu.SemaphoreType.DMA((N_PARTS,)),
            pltpu.SemaphoreType.DMA((N_PARTS,)),
            pltpu.SemaphoreType.DMA((2,)),
            pltpu.SemaphoreType.REGULAR,
        ],
        compiler_params=pltpu.CompilerParams(collective_id=0, has_side_effects=True, vmem_limit_bytes=VMEM_LIMIT),
        name="channels",
    )(voltages, delays, dead_inputs, filter_taps, *tables)

    return pl.pallas_call(
        functools.partial(correlate_kernel, scale),
        out_shape=jax.ShapeDtypeStruct((1, signals, signals), jnp.bfloat16),
        in_specs=[in_hbm, in_hbm],
        out_specs=in_hbm,
        scratch_shapes=[
            pltpu.VMEM((signals, 2 * R), jnp.bfloat16),
            pltpu.VMEM((last_block, 2 * R), jnp.bfloat16),
            pltpu.VMEM((signals // last_block, signals, last_block), jnp.bfloat16),
            pltpu.VMEM((signals // last_block, signals, last_block), jnp.bfloat16),
            pltpu.SemaphoreType.DMA,
            pltpu.SemaphoreType.DMA((signals // last_block,)),
            pltpu.SemaphoreType.DMA((signals // last_block,)),
        ],
        compiler_params=pltpu.CompilerParams(vmem_limit_bytes=VMEM_LIMIT),
        name="correlate",
    )(late, early_sums)


def solution(mesh):
    in_specs = (P("chan", "tm"), P(), P("chan"), P("chan"))
    out_specs = P(("tm", "chan"), None, None)
    return jax.shard_map(shards, mesh=mesh, in_specs=in_specs, out_specs=out_specs, check_vma=False)
```
